128 devices in a mesh: wide: 32 (over y, z, core), narrow: 4 (over x).
Axes of the slice: x: 4, y: 4, z: 4, core: 2. Of those that a mesh axis runs over, the one named last changes fastest.
Arguments:
- weight: bfloat16 [44544, 14848], P('wide', 'narrow'), may hold values from -36 to 36
- sketch: bfloat16 [14848, 256], P('narrow', 'wide'), may hold values from -4 to 4
Outputs:
- coefficients: bfloat16 [256, 14848], P('wide', 'narrow')
- residual: bfloat16 [44544, 14848], P('wide', 'narrow')
The draws below stay inside these ranges and needn't reach their ends.
All inputs are finite; a program needn't handle non-finite values.
Results may differ from the reference program's by a relative error of at most 0.0034.
Values may be sent and summed in bfloat16 or wider, within the bound.
A program may use at most 64 MiB of HBM per device.

```python
import jax
import jax.numpy as jnp
from jax import lax

HID = 44544
DIM = 14848
RANK = 256
ITERS = 6


def draw_weight(key, part):
    key = jax.random.fold_in(key, 11)
    key_entries, key_rows, key_cols = jax.random.split(key, 3)
    entries = jax.random.truncated_normal(key_entries, -4.0, 4.0, (HID, DIM), jnp.float32)
    low, high = (0.3, 3.0)
    row_scale = jnp.exp(jax.random.uniform(key_rows, (HID, 1), jnp.float32, jnp.log(low), jnp.log(high)))
    col_scale = jnp.exp(jax.random.uniform(key_cols, (1, DIM), jnp.float32, jnp.log(low), jnp.log(high)))
    return (entries * row_scale * col_scale).astype(jnp.bfloat16)


def block_levels(stream_key, shape, cuts, low, high):
    loudness, own = 1.0, jax.random.fold_in(stream_key, 6)
    for axis_at, parts in cuts:
        draws = jnp.exp(jax.random.uniform(jax.random.fold_in(own, axis_at), (parts,), jnp.float32, low / len(cuts), high / len(cuts)))
        loudness = loudness * jnp.repeat(draws, shape[axis_at] // parts).reshape([-1 if axis == axis_at else 1 for axis in range(len(shape))])
    return loudness


def centred(stream_key, extent, spread, most, cuts=(), held_as=jnp.bfloat16):
    level = block_levels(stream_key, extent, cuts, -0.22, 0.18) if cuts else 1.0
    array = jax.random.normal(stream_key, extent, jnp.float32) * spread * level
    return jnp.minimum(jnp.maximum(array, -most), most).astype(held_as)


def setup_inputs(seed: int = 0) -> dict:
    streams_of = jax.random.split(jax.random.key(seed), 3)
    return {
        "weight": draw_weight(jax.random.fold_in(streams_of[2], 71), 0),
        "sketch": centred(streams_of[1], (DIM, RANK), 1.0, 4.0, ((0, 4), (1, 32))),
    }


def reference(weight, sketch):
    image = jnp.dot(weight, sketch, preferred_element_type=jnp.float32)
    iterate = image / jnp.sqrt(jnp.sum(image * image))
    for step in range(ITERS):
        cross = jnp.dot(iterate.T, iterate, precision=lax.Precision.HIGHEST)
        iterate = 1.5 * iterate - 0.5 * jnp.dot(iterate, cross, precision=lax.Precision.HIGHEST)
    basis = iterate.astype(jnp.bfloat16)
    coefficients = jnp.dot(basis.T, weight, preferred_element_type=jnp.float32).astype(jnp.bfloat16)
    basis_blocks = basis.reshape(8, HID // 8, RANK)
    weight_blocks = weight.reshape(8, HID // 8, DIM)

    def one_block(pair):
        basis_part, weight_part = pair
        product = jnp.dot(basis_part, coefficients, preferred_element_type=jnp.float32)
        return (weight_part.astype(jnp.float32) - product).astype(jnp.bfloat16)
    residual = lax.map(one_block, (basis_blocks, weight_blocks)).reshape(HID, DIM)
    return (coefficients, residual)
```

```python
import jax
import jax.numpy as jnp
from jax import lax
from jax.experimental import pallas as pl
from jax.experimental.pallas import tpu as pltpu
from jax.sharding import PartitionSpec as P

ITERS = 6
RING = 4
RANK = 256
ROWS = 1392
COLS = 3712
PAD = 1408
CHUNK = PAD // RING
HALF = CHUNK // 2
BLK = 16
WIDE = 1920
SKIP = COLS - WIDE
PART_A = 1024
PART_B = WIDE - PART_A
MESH = pl.DeviceIdType.MESH
F32 = jnp.float32
BF16 = jnp.bfloat16


def mod4(value):
    return lax.rem(value, RING)


def split(value):
    high = value.astype(BF16)
    return high, (value - high.astype(F32)).astype(BF16)


def dot(a, b):
    return jnp.dot(a, b, preferred_element_type=F32)


def dot_split(a, b):
    a_high, a_low = split(a)
    b_high, b_low = split(b)
    return dot(a_high, b_high) + (dot(a_high, b_low) + dot(a_low, b_high))


def main_kernel(
    w_hbm,
    sk_ref,
    basis_out,
    coef_out,
    w_ref,
    own_sk,
    mate_sk,
    s_ref,
    part_f,
    part_b,
    img_in,
    img_mid,
    x_high,
    x_low,
    gram,
    total,
    gram_pair,
    gram_x,
    gram_y,
    gram_z,
    poly,
    basis,
    basis_t,
    mate_send,
    mate_recv,
    sum_f,
    sum_b,
    rs_in,
    rs_mid,
    row_f,
    row_b,
    col_in_a,
    col_in_b,
    col_mid_a,
    col_mid_b,
    coef,
    local_sem,
    send_sem,
    recv_sem,
):
    wide = lax.axis_index("wide")
    x = lax.axis_index("narrow")
    core = lax.rem(wide, 2)
    chip = wide // 2
    y, z = chip // RING, lax.rem(chip, RING)
    s1, s2 = 1 + 3 * core, 4 - 3 * core
    p1, p2 = z + core * (y - z), y + core * (z - y)
    mate = {"wide": chip * 2 + 1 - core}

    def chip_peer(a1, a2):
        return {"wide": (a1 * s1 + a2 * s2) * 2 + core}

    def y_peer(step):
        return {"wide": (mod4(y + step) * RING + z) * 2 + core}

    def z_peer(step):
        return {"wide": (y * RING + mod4(z + step)) * 2 + core}

    def x_peer(step):
        return {"narrow": mod4(x + step)}

    load_w = pltpu.make_async_copy(w_hbm, w_ref.at[pl.ds(0, ROWS)], local_sem.at[0])
    load_w.start()

    barrier = pltpu.get_barrier_semaphore()
    peers = [mate] + [f(s) for f in (x_peer, y_peer, z_peer) for s in (1, 2, 3)]
    for peer in peers:
        pl.semaphore_signal(barrier, inc=1, device_id=peer, device_id_type=MESH)
    own_sk[...] = sk_ref[...].astype(F32)
    w_ref[pl.ds(ROWS, PAD - ROWS), :] = jnp.zeros((PAD - ROWS, COLS), BF16)
    pl.semaphore_wait(barrier, len(peers))

    count = [0]
    pending = []

    def send(src, dst, peer):
        at = count[0]
        count[0] += 1
        copy = pltpu.make_async_remote_copy(
            src_ref=src,
            dst_ref=dst,
            send_sem=send_sem.at[at],
            recv_sem=recv_sem.at[at],
            device_id=peer,
            device_id_type=MESH,
        )
        copy.start()
        pending.append(copy)
        return copy

    def drain():
        for copy in pending:
            copy.wait_send()
        pending.clear()

    def gather16(buf, off, u, v):
        (pu, su), (pv, sv) = u, v

        def blk(au, av, start=0, width=WIDE):
            rows = pl.ds(pl.multiple_of((au * su + av * sv) * BLK, BLK), BLK)
            return buf.at[rows, pl.ds(pl.multiple_of(off + start, 128), width)]

        def at_u(step):
            return {"wide": (mod4(pu + step) * su + pv * sv) * 2 + core}

        def at_v(step):
            return {"wide": (pu * su + mod4(pv + step) * sv) * 2 + core}

        def both(au):
            block = blk(au, pv)
            return send(block, block, at_v(1)), send(block, block, at_v(3))

        own = blk(pu, pv)
        to_right = send(own, own, at_u(1))
        to_left = send(own, own, at_u(3))
        lines = [both(pu)]
        to_right.wait_recv()
        left = blk(mod4(pu + 3), pv, 0, PART_A)
        opp_a = send(left, left, at_u(1))
        lines.append(both(mod4(pu + 3)))
        to_left.wait_recv()
        right = blk(mod4(pu + 1), pv, PART_A, PART_B)
        opp_b = send(right, right, at_u(3))
        lines.append(both(mod4(pu + 1)))
        order = [pu, mod4(pu + 3), mod4(pu + 1), mod4(pu + 2)]
        last = []

        def forward(j):
            rightward, leftward = lines[j]
            if j % 2 == 0:
                rightward.wait_recv()
                block = blk(order[j], mod4(pv + 3))
                last.append(send(block, block, at_v(1)))
                last.append(leftward)
            else:
                leftward.wait_recv()
                block = blk(order[j], mod4(pv + 1))
                last.append(send(block, block, at_v(3)))
                last.append(rightward)

        forward(0)
        opp_a.wait_recv()
        opp_b.wait_recv()
        lines.append(both(mod4(pu + 2)))
        forward(1)
        forward(2)
        forward(3)
        for copy in last:
            copy.wait_recv()
        drain()

    axis1, axis2 = (p1, s1), (p2, s2)
    my_off = core * SKIP
    only_off = core * WIDE
    mate_off = (1 - core) * SKIP

    my_cols = pl.ds(pl.multiple_of(my_off, 128), WIDE)
    first = send(own_sk.at[:, pl.ds(pl.multiple_of(mate_off, 128), WIDE)], mate_sk, mate)
    first.wait_recv()
    mine, other = own_sk[:, my_cols], mate_sk[...]
    even = core == 0
    pair = jnp.concatenate([jnp.where(even, mine, other), jnp.where(even, other, mine)], axis=0)
    s_ref[pl.ds(pl.multiple_of(chip * BLK, BLK), BLK), my_cols] = pair.astype(BF16)
    gather16(s_ref, my_off, axis1, axis2)
    half = s_ref.at[:, pl.ds(pl.multiple_of(only_off, 128), SKIP)]
    swap = send(half, half, mate)
    load_w.wait()
    swap.wait_recv()
    drain()

    def chunk_rows(step):
        return pl.multiple_of(mod4(x + step) * CHUNK, 16)

    def image_chunk(step):
        start = chunk_rows(step)
        value = lax.dot_general(
            w_ref[pl.ds(start, CHUNK), :],
            s_ref[...],
            (((1,), (1,)), ((), ())),
            preferred_element_type=F32,
        )
        part_f[pl.ds(start, CHUNK), :] = value
        part_b[pl.ds(start, CHUNK), :] = value.astype(BF16)

    def half_rows(step, second):
        return pl.ds(pl.multiple_of(chunk_rows(step) + second * HALF, 16), HALF)

    image_chunk(2)
    in0 = send(part_b.at[half_rows(2, 0)], img_in.at[0], x_peer(1))
    in1 = send(part_b.at[half_rows(2, 1)], img_in.at[1], x_peer(3))
    image_chunk(1)
    in2 = send(part_b.at[half_rows(1, 1)], img_in.at[2], x_peer(1))
    image_chunk(3)
    in3 = send(part_b.at[half_rows(3, 0)], img_in.at[3], x_peer(3))
    in0.wait_recv()
    img_mid[0] = (part_f[half_rows(1, 0), :] + img_in[0].astype(F32)).astype(BF16)
    in4 = send(img_mid.at[0], img_in.at[4], x_peer(1))
    in1.wait_recv()
    img_mid[1] = (part_f[half_rows(3, 1), :] + img_in[1].astype(F32)).astype(BF16)
    in5 = send(img_mid.at[1], img_in.at[5], x_peer(3))
    image_chunk(0)
    in3.wait_recv()
    in2.wait_recv()
    in4.wait_recv()
    half_a = part_f[half_rows(0, 0), :] + img_in[3].astype(F32) + img_in[4].astype(F32)
    in5.wait_recv()
    half_b = part_f[half_rows(0, 1), :] + img_in[2].astype(F32) + img_in[5].astype(F32)
    own_high, own_low = split(jnp.concatenate([half_a, half_b], axis=0))
    x_high[pl.ds(chunk_rows(0), CHUNK), :] = own_high
    x_low[pl.ds(chunk_rows(0), CHUNK), :] = own_low
    drain()

    def gram_dot(a, b):
        return lax.dot_general(a, b, (((0,), (0,)), ((), ())), preferred_element_type=F32)

    gram[...] = gram_dot(own_high, own_high) + (
        gram_dot(own_high, own_low) + gram_dot(own_low, own_high)
    )
    g_core = pl.multiple_of(core * 128, 128)
    g_mate = pl.multiple_of((1 - core) * 128, 128)
    copy = send(gram.at[pl.ds(g_mate, 128)], gram_pair, mate)
    copy.wait_recv()
    gram[pl.ds(g_core, 128), :] = gram[pl.ds(g_core, 128), :] + gram_pair[...]

    def gram_rows(ax, ay, rows):
        return pl.ds(pl.multiple_of(core * 128 + ax * 32 + ay * 8, 8), rows)

    copies = [
        send(gram.at[gram_rows(mod4(x + s), 0, 32)], gram_x.at[s - 1], x_peer(s)) for s in (1, 2, 3)
    ]
    for copy in copies:
        copy.wait_recv()
    at_x = gram_rows(x, 0, 32)
    gram[at_x, :] = gram[at_x, :] + gram_x[0] + gram_x[1] + gram_x[2]

    def gather_x(buf):
        mine = buf.at[pl.ds(chunk_rows(0), CHUNK)]
        rightward = send(mine, mine, x_peer(1))
        leftward = send(mine, mine, x_peer(3))

        def middle():
            rightward.wait_recv()
            piece = buf.at[half_rows(3, 0)]
            a = send(piece, piece, x_peer(1))
            leftward.wait_recv()
            piece = buf.at[half_rows(1, 1)]
            b = send(piece, piece, x_peer(3))

            def end():
                a.wait_recv()
                b.wait_recv()

            return end

        return middle

    high_middle = gather_x(x_high)
    copies = [
        send(gram.at[gram_rows(x, mod4(y + s), 8)], gram_y.at[s - 1], y_peer(s)) for s in (1, 2, 3)
    ]
    for copy in copies:
        copy.wait_recv()
    at_y = gram_rows(x, y, 8)
    gram[at_y, :] = gram[at_y, :] + gram_y[0] + gram_y[1] + gram_y[2]
    copies = [send(gram.at[at_y], gram_z.at[s - 1], z_peer(s)) for s in (1, 2, 3)]
    for copy in copies:
        copy.wait_recv()
    total[at_y, :] = gram[at_y, :] + gram_z[0] + gram_z[1] + gram_z[2]
    copies = [send(total.at[at_y], total.at[at_y], y_peer(s)) for s in (1, 2, 3)]
    high_end = high_middle()
    for copy in copies:
        copy.wait_recv()
    copies = [send(total.at[at_x], total.at[at_x], x_peer(s)) for s in (1, 2, 3)]
    for copy in copies:
        copy.wait_recv()
    rows = pl.ds(g_core, 128)
    copy = send(total.at[rows], total.at[rows], mate)
    low_middle = gather_x(x_low)
    copy.wait_recv()

    whole = total[...]
    diagonal = lax.broadcasted_iota(jnp.int32, (RANK, RANK), 0) == lax.broadcasted_iota(
        jnp.int32, (RANK, RANK), 1
    )
    trace = jnp.sum(jnp.where(diagonal, whole, 0.0), keepdims=True)
    poly[pl.ds(0, RANK), :] = whole / trace
    poly[pl.ds(RANK, RANK), :] = jnp.where(diagonal, 1.0 / jnp.sqrt(trace), 0.0)

    def factor(g):
        return jnp.where(diagonal, 1.5, 0.0) - 0.5 * g

    def iteration(_, carry):
        both = poly[...]
        p = factor(both[:RANK])
        p_high, p_low = split(p)

        def times_p(a):
            a_high, a_low = split(a)
            return dot(a_high, p_high) + (dot(a_high, p_low) + dot(a_low, p_high))

        both = times_p(both)
        poly[pl.ds(RANK, RANK), :] = both[RANK:]
        poly[pl.ds(0, RANK), :] = times_p(both[:RANK])
        return carry

    lax.fori_loop(0, ITERS - 1, iteration, 0)
    low_end = low_middle()
    high_end()
    q = dot_split(poly[pl.ds(RANK, RANK), :], factor(poly[pl.ds(0, RANK), :]))
    q_high, q_low = split(q)
    low_end()

    basis[...] = (
        dot(x_high[...], q_high) + (dot(x_high[...], q_low) + dot(x_low[...], q_high))
    ).astype(BF16)
    save_basis = pltpu.make_async_copy(basis.at[pl.ds(0, ROWS)], basis_out, local_sem.at[1])
    save_basis.start()
    basis_t[...] = basis[...].T

    def partial(off, start, width):
        cols = pl.ds(pl.multiple_of(off + start, 128), width)
        return dot(basis_t[...], w_ref[:, cols])

    def cols(part):
        return pl.ds(0, PART_A) if part == 0 else pl.ds(PART_A, PART_B)

    copies = []
    for part, (start, width) in enumerate(((0, PART_A), (PART_A, PART_B))):
        mate_send[:, cols(part)] = partial(mate_off, start, width).astype(BF16)
        copies.append(send(mate_send.at[:, cols(part)], mate_recv.at[:, cols(part)], mate))
    for part, (start, width) in enumerate(((0, PART_A), (PART_A, PART_B))):
        value = partial(my_off, start, width)
        copies[part].wait_recv()
        value = value + mate_recv[:, cols(part)].astype(F32)
        sum_f[:, cols(part)] = value
        sum_b[:, cols(part)] = value.astype(BF16)

    def rows_of(a1, a2):
        return pl.ds(pl.multiple_of((a1 * s1 + a2 * s2) * BLK, BLK), BLK)

    u1, u2, u3 = mod4(p1 + 1), mod4(p1 + 2), mod4(p1 + 3)
    right1, left1 = chip_peer(u1, p2), chip_peer(u3, p2)
    in0 = [send(sum_b.at[rows_of(u2, v)], rs_in.at[0, v], right1) for v in (0, 1)]
    in1 = [send(sum_b.at[rows_of(u2, v + 2)], rs_in.at[1, v], left1) for v in (0, 1)]
    in2 = [send(sum_b.at[rows_of(u1, v + 2)], rs_in.at[2, v], right1) for v in (0, 1)]
    in3 = [send(sum_b.at[rows_of(u3, v)], rs_in.at[3, v], left1) for v in (0, 1)]
    in4, in5 = [], []
    for v in (0, 1):
        in0[v].wait_recv()
        rs_mid[0, v] = (sum_f[rows_of(u1, v), :] + rs_in[0, v].astype(F32)).astype(BF16)
        in4.append(send(rs_mid.at[0, v], rs_in.at[4, v], right1))
        in1[v].wait_recv()
        rs_mid[1, v] = (sum_f[rows_of(u3, v + 2), :] + rs_in[1, v].astype(F32)).astype(BF16)
        in5.append(send(rs_mid.at[1, v], rs_in.at[5, v], left1))
    for v in (0, 1):
        in3[v].wait_recv()
        in4[v].wait_recv()
        value = sum_f[rows_of(p1, v), :] + rs_in[3, v].astype(F32) + rs_in[4, v].astype(F32)
        row_f[v] = value
        row_b[v] = value.astype(BF16)
        in2[v].wait_recv()
        in5[v].wait_recv()
        value = sum_f[rows_of(p1, v + 2), :] + rs_in[2, v].astype(F32) + rs_in[5, v].astype(F32)
        row_f[v + 2] = value
        row_b[v + 2] = value.astype(BF16)

    v1, v2, v3 = mod4(p2 + 1), mod4(p2 + 2), mod4(p2 + 3)
    right2, left2 = chip_peer(p1, v1), chip_peer(p1, v3)
    ca, cb = cols(0), cols(1)
    in0 = send(row_b.at[v2, :, ca], col_in_a.at[0], right2)
    in1 = send(row_b.at[v2, :, cb], col_in_b.at[0], left2)
    in2 = send(row_b.at[v1, :, cb], col_in_b.at[1], right2)
    in3 = send(row_b.at[v3, :, ca], col_in_a.at[1], left2)
    in0.wait_recv()
    col_mid_a[...] = (row_f[v1, :, ca] + col_in_a[0].astype(F32)).astype(BF16)
    in4 = send(col_mid_a, col_in_a.at[2], right2)
    in1.wait_recv()
    col_mid_b[...] = (row_f[v3, :, cb] + col_in_b[0].astype(F32)).astype(BF16)
    in5 = send(col_mid_b, col_in_b.at[2], left2)
    in3.wait_recv()
    in4.wait_recv()
    my_rows = pl.ds(pl.multiple_of(chip * BLK, BLK), BLK)
    coef[my_rows, pl.ds(pl.multiple_of(my_off, 128), PART_A)] = (
        row_f[p2, :, ca] + col_in_a[1].astype(F32) + col_in_a[2].astype(F32)
    ).astype(BF16)
    in2.wait_recv()
    in5.wait_recv()
    coef[my_rows, pl.ds(pl.multiple_of(my_off + PART_A, 128), PART_B)] = (
        row_f[p2, :, cb] + col_in_b[1].astype(F32) + col_in_b[2].astype(F32)
    ).astype(BF16)
    drain()

    gather16(coef, my_off, axis2, axis1)
    half = coef.at[:, pl.ds(pl.multiple_of(only_off, 128), SKIP)]
    swap = send(half, half, mate)
    swap.wait_recv()
    drain()
    save_coef = pltpu.make_async_copy(coef, coef_out, local_sem.at[2])
    save_coef.start()
    save_basis.wait()
    save_coef.wait()
    assert count[0] <= COPIES, count[0]


COPIES = 128


def residual_kernel(w_ref, basis_ref, coef_ref, residual_ref, own_ref):
    @pl.when(pl.program_id(0) == 0)
    def _():
        wide = lax.axis_index("wide")
        block = coef_ref[pl.ds(pl.multiple_of((wide // 2) * BLK, BLK), BLK), :].astype(F32)
        first = lax.rem(wide, 2) == 0
        own_ref[...] = jnp.where(first, block[:8], block[8:]).astype(BF16)

    product = dot(basis_ref[...], coef_ref[...])
    residual_ref[...] = (w_ref[...].astype(F32) - product).astype(BF16)


def shards(weight, sketch):
    basis, coef = pl.pallas_call(
        main_kernel,
        out_shape=(
            jax.ShapeDtypeStruct((ROWS, RANK), BF16),
            jax.ShapeDtypeStruct((RANK, COLS), BF16),
        ),
        in_specs=[pl.BlockSpec(memory_space=pl.ANY), pl.BlockSpec(memory_space=pltpu.VMEM)],
        out_specs=[pl.BlockSpec(memory_space=pl.ANY)] * 2,
        scratch_shapes=[
            pltpu.VMEM((PAD, COLS), BF16),
            pltpu.VMEM((8, COLS), F32),
            pltpu.VMEM((8, WIDE), F32),
            pltpu.VMEM((RANK, COLS), BF16),
            pltpu.VMEM((PAD, RANK), F32),
            pltpu.VMEM((PAD, RANK), BF16),
            pltpu.VMEM((6, HALF, RANK), BF16),
            pltpu.VMEM((2, HALF, RANK), BF16),
            pltpu.VMEM((PAD, RANK), BF16),
            pltpu.VMEM((PAD, RANK), BF16),
            pltpu.VMEM((RANK, RANK), F32),
            pltpu.VMEM((RANK, RANK), F32),
            pltpu.VMEM((128, RANK), F32),
            pltpu.VMEM((3, 32, RANK), F32),
            pltpu.VMEM((3, 8, RANK), F32),
            pltpu.VMEM((3, 8, RANK), F32),
            pltpu.VMEM((2 * RANK, RANK), F32),
            pltpu.VMEM((PAD, RANK), BF16),
            pltpu.VMEM((RANK, PAD), BF16),
            pltpu.VMEM((RANK, WIDE), BF16),
            pltpu.VMEM((RANK, WIDE), BF16),
            pltpu.VMEM((RANK, WIDE), F32),
            pltpu.VMEM((RANK, WIDE), BF16),
            pltpu.VMEM((6, 2, BLK, WIDE), BF16),
            pltpu.VMEM((2, 2, BLK, WIDE), BF16),
            pltpu.VMEM((4, BLK, WIDE), F32),
            pltpu.VMEM((4, BLK, WIDE), BF16),
            pltpu.VMEM((3, BLK, PART_A), BF16),
            pltpu.VMEM((3, BLK, PART_B), BF16),
            pltpu.VMEM((BLK, PART_A), BF16),
            pltpu.VMEM((BLK, PART_B), BF16),
            pltpu.VMEM((RANK, COLS), BF16),
            pltpu.SemaphoreType.DMA((3,)),
            pltpu.SemaphoreType.DMA((COPIES,)),
            pltpu.SemaphoreType.DMA((COPIES,)),
        ],
        compiler_params=pltpu.CompilerParams(
            collective_id=0, has_side_effects=True, vmem_limit_bytes=44 * 1024 * 1024
        ),
        cost_estimate=pl.CostEstimate(
            flops=2 * 2 * ROWS * COLS * RANK, bytes_accessed=2 * ROWS * COLS, transcendentals=0
        ),
        name="polar_basis",
    )(weight, sketch.T)

    rows = 240
    residual, own = pl.pallas_call(
        residual_kernel,
        grid=(pl.cdiv(ROWS, rows),),
        out_shape=(
            jax.ShapeDtypeStruct((ROWS, COLS), BF16),
            jax.ShapeDtypeStruct((8, COLS), BF16),
        ),
        in_specs=[
            pl.BlockSpec((rows, COLS), lambda i: (i, 0)),
            pl.BlockSpec((rows, RANK), lambda i: (i, 0)),
            pl.BlockSpec((RANK, COLS), lambda i: (0, 0)),
        ],
        out_specs=[
            pl.BlockSpec((rows, COLS), lambda i: (i, 0)),
            pl.BlockSpec((8, COLS), lambda i: (0, 0)),
        ],
        compiler_params=pltpu.CompilerParams(vmem_limit_bytes=24 * 1024 * 1024),
        cost_estimate=pl.CostEstimate(
            flops=2 * ROWS * COLS * RANK, bytes_accessed=4 * ROWS * COLS, transcendentals=0
        ),
        name="residual",
    )(weight, basis, coef)
    return own, residual


def solution(mesh):
    placed = (P("wide", "narrow"), P("narrow", "wide"))
    return jax.shard_map(
        shards,
        mesh=mesh,
        in_specs=placed,
        out_specs=(P("wide", "narrow"), P("wide", "narrow")),
        check_vma=False,
    )
```

```python
import jax
import jax.numpy as jnp
from jax import lax
from jax.experimental import pallas as pl
from jax.experimental.pallas import tpu as pltpu
from jax.sharding import PartitionSpec as P

ITERS = 6
RING = 4
RANK = 256
ROWS = 1392
COLS = 3712
PAD = 1408
CHUNK = PAD // RING
HALF = CHUNK // 2
BLK = 16
WIDE = 1920
SKIP = COLS - WIDE
TILES = 16
SKIP2 = COLS - TILES * 128
PART = TILES * 64
MESH = pl.DeviceIdType.MESH
F32 = jnp.float32
BF16 = jnp.bfloat16


def mod4(value):
    return lax.rem(value, RING)


def split(value):
    high = value.astype(BF16)
    return high, (value - high.astype(F32)).astype(BF16)


def dot(a, b):
    return jnp.dot(a, b, preferred_element_type=F32)


def dot_split(a, b):
    a_high, a_low = split(a)
    b_high, b_low = split(b)
    return dot(a_high, b_high) + (dot(a_high, b_low) + dot(a_low, b_high))


def main_kernel(
    w_hbm,
    sk_ref,
    basis_out,
    coef_out,
    w_ref,
    own_sk,
    mate_sk,
    s_ref,
    part_f,
    part_b,
    img_in,
    img_mid,
    gram,
    total,
    gram_pair,
    gram_x,
    gram_y,
    gram_z,
    poly,
    basis,
    img,
    img_t,
    mate_send,
    mate_recv,
    z_f,
    z_b,
    z_in,
    row_f,
    row_b,
    col_in,
    coef,
    coef_mate,
    local_sem,
    send_sem,
    recv_sem,
):
    wide = lax.axis_index("wide")
    x = lax.axis_index("narrow")
    core = lax.rem(wide, 2)
    chip = wide // 2
    y, z = chip // RING, lax.rem(chip, RING)
    s1, s2 = 1 + 3 * core, 4 - 3 * core
    p1, p2 = z + core * (y - z), y + core * (z - y)
    mate = {"wide": chip * 2 + 1 - core}

    def chip_peer(a1, a2):
        return {"wide": (a1 * s1 + a2 * s2) * 2 + core}

    def y_peer(step):
        return {"wide": (mod4(y + step) * RING + z) * 2 + core}

    def z_peer(step):
        return {"wide": (y * RING + mod4(z + step)) * 2 + core}

    def x_peer(step):
        return {"narrow": mod4(x + step)}

    load_w = pltpu.make_async_copy(w_hbm, w_ref.at[pl.ds(0, ROWS)], local_sem.at[0])
    load_w.start()

    barrier = pltpu.get_barrier_semaphore()
    peers = [mate] + [f(s) for f in (x_peer, y_peer, z_peer) for s in (1, 2, 3)]
    for peer in peers:
        pl.semaphore_signal(barrier, inc=1, device_id=peer, device_id_type=MESH)
    own_sk[...] = sk_ref[...].astype(F32)
    w_ref[pl.ds(ROWS, PAD - ROWS), :] = jnp.zeros((PAD - ROWS, COLS), BF16)
    pl.semaphore_wait(barrier, len(peers))

    count = [0]
    pending = []

    def send(src, dst, peer):
        at = count[0]
        count[0] += 1
        copy = pltpu.make_async_remote_copy(
            src_ref=src,
            dst_ref=dst,
            send_sem=send_sem.at[at],
            recv_sem=recv_sem.at[at],
            device_id=peer,
            device_id_type=MESH,
        )
        copy.start()
        pending.append(copy)
        return copy

    def drain():
        for copy in pending:
            copy.wait_send()
        pending.clear()

    def gather16(blk, u, v, share):
        (pu, su), (pv, sv) = u, v

        def at_u(step):
            return {"wide": (mod4(pu + step) * su + pv * sv) * 2 + core}

        def at_v(step):
            return {"wide": (pu * su + mod4(pv + step) * sv) * 2 + core}

        own = blk(pu, pv)
        along_u = {s: send(own, own, at_u(s)) for s in (2, 1, 3)}
        along_v = [(pu, {s: send(own, own, at_v(s)) for s in (2, 1, 3)})]
        shared = [share(pu, pv)]
        for s in (1, 3, 2):
            along_u[s].wait_recv()
            a = mod4(pu + 4 - s)
            block = blk(a, pv)
            along_v.append((a, {t: send(block, block, at_v(t)) for t in (2, 1, 3)}))
            shared.append(share(a, pv))
        for a, copies in along_v:
            for t in (1, 3, 2):
                copies[t].wait_recv()
                shared.append(share(a, mod4(pv + 4 - t)))
        for copy in shared:
            copy.wait_recv()
        drain()

    axis1, axis2 = (p1, s1), (p2, s2)
    my_off = core * SKIP
    only_off = core * WIDE
    mate_off = (1 - core) * SKIP
    my_off2, mate_off2 = core * SKIP2, (1 - core) * SKIP2

    my_cols = pl.ds(pl.multiple_of(my_off, 128), WIDE)
    first = send(own_sk.at[:, pl.ds(pl.multiple_of(mate_off, 128), WIDE)], mate_sk, mate)
    first.wait_recv()
    mine, other = own_sk[:, my_cols], mate_sk[...]
    even = core == 0
    pair = jnp.concatenate([jnp.where(even, mine, other), jnp.where(even, other, mine)], axis=0)
    s_ref[pl.ds(pl.multiple_of(chip * BLK, BLK), BLK), my_cols] = pair.astype(BF16)

    def sketch_block(a1, a2):
        return s_ref.at[pl.ds(pl.multiple_of((a1 * s1 + a2 * s2) * BLK, BLK), BLK), my_cols]

    def share_sketch(a1, a2):
        rows = pl.ds(pl.multiple_of((a1 * s1 + a2 * s2) * BLK, BLK), BLK)
        block = s_ref.at[rows, pl.ds(pl.multiple_of(only_off, 128), SKIP)]
        return send(block, block, mate)

    gather16(sketch_block, axis1, axis2, share_sketch)
    load_w.wait()

    def chunk_rows(step):
        return pl.multiple_of(mod4(x + step) * CHUNK, 16)

    def image_chunk(step):
        start = chunk_rows(step)
        value = lax.dot_general(
            w_ref[pl.ds(start, CHUNK), :],
            s_ref[...],
            (((1,), (1,)), ((), ())),
            preferred_element_type=F32,
        )
        part_f[pl.ds(start, CHUNK), :] = value
        part_b[pl.ds(start, CHUNK), :] = value.astype(BF16)

    def half_rows(step, second):
        return pl.ds(pl.multiple_of(chunk_rows(step) + second * HALF, 16), HALF)

    image_chunk(2)
    in0 = send(part_b.at[half_rows(2, 0)], img_in.at[0], x_peer(1))
    in1 = send(part_b.at[half_rows(2, 1)], img_in.at[1], x_peer(3))
    image_chunk(1)
    in2 = send(part_b.at[half_rows(1, 1)], img_in.at[2], x_peer(1))
    image_chunk(3)
    in3 = send(part_b.at[half_rows(3, 0)], img_in.at[3], x_peer(3))
    in0.wait_recv()
    img_mid[0] = (part_f[half_rows(1, 0), :] + img_in[0].astype(F32)).astype(BF16)
    in4 = send(img_mid.at[0], img_in.at[4], x_peer(1))
    in1.wait_recv()
    img_mid[1] = (part_f[half_rows(3, 1), :] + img_in[1].astype(F32)).astype(BF16)
    in5 = send(img_mid.at[1], img_in.at[5], x_peer(3))
    image_chunk(0)
    in3.wait_recv()
    in4.wait_recv()
    own_a, own_b = half_rows(0, 0), half_rows(0, 1)
    img[own_a, :] = (part_f[own_a, :] + img_in[3].astype(F32) + img_in[4].astype(F32)).astype(BF16)
    a_right = send(img.at[own_a], img.at[own_a], x_peer(1))
    in2.wait_recv()
    in5.wait_recv()
    img[own_b, :] = (part_f[own_b, :] + img_in[2].astype(F32) + img_in[5].astype(F32)).astype(BF16)
    b_left = send(img.at[own_b], img.at[own_b], x_peer(3))
    b_right = send(img.at[own_b], img.at[own_b], x_peer(1))
    a_left = send(img.at[own_a], img.at[own_a], x_peer(3))

    own = img[pl.ds(chunk_rows(0), CHUNK), :]
    gram[...] = lax.dot_general(own, own, (((0,), (0,)), ((), ())), preferred_element_type=F32)
    g_core = pl.multiple_of(core * 128, 128)
    g_mate = pl.multiple_of((1 - core) * 128, 128)
    copy = send(gram.at[pl.ds(g_mate, 128)], gram_pair, mate)
    copy.wait_recv()
    gram[pl.ds(g_core, 128), :] = gram[pl.ds(g_core, 128), :] + gram_pair[...]

    def gram_rows(ax):
        return pl.ds(pl.multiple_of(core * 128 + ax * 32, 32), 32)

    at_x = gram_rows(x)
    gram_stage = {s: send(gram.at[gram_rows(mod4(x + s))], gram_x.at[s - 1], x_peer(s)) for s in (2, 1, 3)}
    a_right.wait_recv()
    piece = img.at[half_rows(3, 0)]
    opp_a = send(piece, piece, x_peer(1))
    b_left.wait_recv()
    piece = img.at[half_rows(1, 1)]
    opp_b = send(piece, piece, x_peer(3))
    for copy in gram_stage.values():
        copy.wait_recv()
    gram_z[0] = gram[at_x, :] + gram_x[0] + gram_x[1] + gram_x[2]
    gram_stage = [send(gram_z.at[0], gram_z.at[s], z_peer(s)) for s in (2, 1, 3)]
    for copy in (a_left, b_right, opp_a, opp_b):
        copy.wait_recv()

    img_t[...] = img[...].T

    def partial(off, part):
        cols = pl.ds(pl.multiple_of(off + part * PART, 128), PART)
        return dot(img_t[...], w_ref[:, cols])

    copies = []
    for part in (0, 1):
        mate_send[part] = partial(mate_off2, part).astype(BF16)
        copies.append(send(mate_send.at[part], mate_recv.at[part], mate))
    for copy in gram_stage:
        copy.wait_recv()
    gram_y[0] = gram_z[0] + gram_z[1] + gram_z[2] + gram_z[3]
    gram_stage = [send(gram_y.at[0], gram_y.at[s], y_peer(s)) for s in (2, 1, 3)]
    for part in (0, 1):
        value = partial(my_off2, part)
        copies[part].wait_recv()
        value = value + mate_recv[part].astype(F32)
        for tile in range(PART // 128):
            block = value[:, tile * 128 : tile * 128 + 128]
            z_f[part * (PART // 128) + tile] = block
            z_b[part * (PART // 128) + tile] = block.astype(BF16)

    scatter = {}
    for s in (2, 1, 3):
        a1 = mod4(p1 + s)
        for a2 in range(RING):
            scatter[s, a2] = send(z_b.at[a1 * s1 + a2 * s2], z_in.at[s - 1, a2], chip_peer(a1, p2))
    for copy in gram_stage:
        copy.wait_recv()
    total[at_x, :] = gram_y[0] + gram_y[1] + gram_y[2] + gram_y[3]
    gram_stage = [send(total.at[at_x], total.at[at_x], x_peer(s)) for s in (2, 1, 3)]
    for copy in gram_stage:
        copy.wait_recv()
    rows = pl.ds(g_core, 128)
    copy = send(total.at[rows], total.at[rows], mate)
    copy.wait_recv()

    whole = total[...]
    diagonal = lax.broadcasted_iota(jnp.int32, (RANK, RANK), 0) == lax.broadcasted_iota(
        jnp.int32, (RANK, RANK), 1
    )
    trace = jnp.sum(jnp.where(diagonal, whole, 0.0), keepdims=True)
    poly[pl.ds(0, RANK), :] = whole / trace
    poly[pl.ds(RANK, RANK), :] = jnp.where(diagonal, 1.0 / jnp.sqrt(trace), 0.0)

    def factor(g):
        return jnp.where(diagonal, 1.5, 0.0) - 0.5 * g

    def iteration(_, carry):
        both = poly[...]
        p = factor(both[:RANK])
        p_high, p_low = split(p)

        def times_p(a):
            a_high, a_low = split(a)
            return dot(a_high, p_high) + (dot(a_high, p_low) + dot(a_low, p_high))

        both = times_p(both)
        poly[pl.ds(RANK, RANK), :] = both[RANK:]
        poly[pl.ds(0, RANK), :] = times_p(both[:RANK])
        return carry

    lax.fori_loop(0, 2, iteration, 0)

    def row_sum(a2):
        for s in (1, 2, 3):
            scatter[s, a2].wait_recv()

    for a2 in range(RING):
        row_sum(a2)
        value = z_f[p1 * s1 + a2 * s2]
        for s in (1, 2, 3):
            value = value + z_in[s - 1, a2].astype(F32)
        row_f[a2] = value
        row_b[a2] = value.astype(BF16)
    column = [
        send(row_b.at[mod4(p2 + s)], col_in.at[s - 1], chip_peer(p1, mod4(p2 + s))) for s in (2, 1, 3)
    ]
    lax.fori_loop(2, ITERS - 1, iteration, 0)
    q = dot_split(poly[pl.ds(RANK, RANK), :], factor(poly[pl.ds(0, RANK), :]))
    for copy in column:
        copy.wait_recv()
    mine = row_f[p2]
    for s in range(3):
        mine = mine + col_in[s].astype(F32)
    coef[chip] = dot_split(q, mine).astype(BF16)

    q_high, q_low = split(q)

    def coef_block(a2, a1):
        return coef.at[a1 * s1 + a2 * s2]

    def share_coef(a2, a1):
        at = a1 * s1 + a2 * s2
        return send(coef.at[at], coef_mate.at[at], mate)

    def basis_rows():
        basis[...] = (dot(img[...], q_high) + dot(img[...], q_low)).astype(BF16)
        save = pltpu.make_async_copy(basis.at[pl.ds(0, ROWS)], basis_out, local_sem.at[1])
        save.start()
        return save

    gather16(coef_block, axis2, axis1, share_coef)
    save_basis = basis_rows()
    save_own = pltpu.make_async_copy(coef, coef_out.at[core], local_sem.at[2])
    save_mate = pltpu.make_async_copy(coef_mate, coef_out.at[1 - core], local_sem.at[3])
    save_own.start()
    save_mate.start()
    save_basis.wait()
    save_own.wait()
    save_mate.wait()
    assert count[0] <= COPIES, count[0]


COPIES = 128


def residual_kernel(w_ref, basis_ref, coef_ref, residual_ref, own_ref, whole):
    @pl.when(pl.program_id(0) == 0)
    def _():
        for tile in range(COLS // 128):
            at = (0, tile) if tile < TILES else (1, tile - SKIP2 // 128)
            whole[:, tile * 128 : tile * 128 + 128] = coef_ref[at]
        wide = lax.axis_index("wide")
        block = whole[pl.ds(pl.multiple_of((wide // 2) * BLK, BLK), BLK), :].astype(F32)
        first = lax.rem(wide, 2) == 0
        own_ref[...] = jnp.where(first, block[:8], block[8:]).astype(BF16)

    product = dot(basis_ref[...], whole[...])
    residual_ref[...] = (w_ref[...].astype(F32) - product).astype(BF16)


def shards(weight, sketch):
    basis, coef = pl.pallas_call(
        main_kernel,
        out_shape=(
            jax.ShapeDtypeStruct((ROWS, RANK), BF16),
            jax.ShapeDtypeStruct((2, TILES, RANK, 128), BF16),
        ),
        in_specs=[pl.BlockSpec(memory_space=pl.ANY), pl.BlockSpec(memory_space=pltpu.VMEM)],
        out_specs=[pl.BlockSpec(memory_space=pl.ANY)] * 2,
        scratch_shapes=[
            pltpu.VMEM((PAD, COLS), BF16),
            pltpu.VMEM((8, COLS), F32),
            pltpu.VMEM((8, WIDE), F32),
            pltpu.VMEM((RANK, COLS), BF16),
            pltpu.VMEM((PAD, RANK), F32),
            pltpu.VMEM((PAD, RANK), BF16),
            pltpu.VMEM((6, HALF, RANK), BF16),
            pltpu.VMEM((2, HALF, RANK), BF16),
            pltpu.VMEM((RANK, RANK), F32),
            pltpu.VMEM((RANK, RANK), F32),
            pltpu.VMEM((128, RANK), F32),
            pltpu.VMEM((3, 32, RANK), F32),
            pltpu.VMEM((4, 32, RANK), F32),
            pltpu.VMEM((4, 32, RANK), F32),
            pltpu.VMEM((2 * RANK, RANK), F32),
            pltpu.VMEM((PAD, RANK), BF16),
            pltpu.VMEM((PAD, RANK), BF16),
            pltpu.VMEM((RANK, PAD), BF16),
            pltpu.VMEM((2, RANK, PART), BF16),
            pltpu.VMEM((2, RANK, PART), BF16),
            pltpu.VMEM((TILES, RANK, 128), F32),
            pltpu.VMEM((TILES, RANK, 128), BF16),
            pltpu.VMEM((3, RING, RANK, 128), BF16),
            pltpu.VMEM((RING, RANK, 128), F32),
            pltpu.VMEM((RING, RANK, 128), BF16),
            pltpu.VMEM((3, RANK, 128), BF16),
            pltpu.VMEM((TILES, RANK, 128), BF16),
            pltpu.VMEM((TILES, RANK, 128), BF16),
            pltpu.SemaphoreType.DMA((4,)),
            pltpu.SemaphoreType.DMA((COPIES,)),
            pltpu.SemaphoreType.DMA((COPIES,)),
        ],
        compiler_params=pltpu.CompilerParams(
            collective_id=0, has_side_effects=True, vmem_limit_bytes=44 * 1024 * 1024
        ),
        cost_estimate=pl.CostEstimate(
            flops=2 * 2 * ROWS * COLS * RANK, bytes_accessed=2 * ROWS * COLS, transcendentals=0
        ),
        name="polar_basis",
    )(weight, sketch.T)

    rows = 240
    residual, own = pl.pallas_call(
        residual_kernel,
        grid=(pl.cdiv(ROWS, rows),),
        out_shape=(
            jax.ShapeDtypeStruct((ROWS, COLS), BF16),
            jax.ShapeDtypeStruct((8, COLS), BF16),
        ),
        in_specs=[
            pl.BlockSpec((rows, COLS), lambda i: (i, 0)),
            pl.BlockSpec((rows, RANK), lambda i: (i, 0)),
            pl.BlockSpec((2, TILES, RANK, 128), lambda i: (0, 0, 0, 0)),
        ],
        out_specs=[
            pl.BlockSpec((rows, COLS), lambda i: (i, 0)),
            pl.BlockSpec((8, COLS), lambda i: (0, 0)),
        ],
        scratch_shapes=[pltpu.VMEM((RANK, COLS), BF16)],
        compiler_params=pltpu.CompilerParams(vmem_limit_bytes=24 * 1024 * 1024),
        cost_estimate=pl.CostEstimate(
            flops=2 * ROWS * COLS * RANK, bytes_accessed=4 * ROWS * COLS, transcendentals=0
        ),
        name="residual",
    )(weight, basis, coef)
    return own, residual


def solution(mesh):
    placed = (P("wide", "narrow"), P("narrow", "wide"))
    return jax.shard_map(
        shards,
        mesh=mesh,
        in_specs=placed,
        out_specs=(P("wide", "narrow"), P("wide", "narrow")),
        check_vma=False,
    )
```

```python
import jax
import jax.numpy as jnp
from jax import lax
from jax.experimental import pallas as pl
from jax.experimental.pallas import tpu as pltpu
from jax.sharding import PartitionSpec as P

ITERS = 6
RING = 4
RANK = 256
ROWS = 1392
COLS = 3712
PAD = 1408
CHUNK = PAD // RING
STREAMS = ((0, 192), (192, 160))
BLK = 16
WIDE = 1920
SKIP = COLS - WIDE
TILES = 16
SKIP2 = COLS - TILES * 128
PART = TILES * 64
MESH = pl.DeviceIdType.MESH
F32 = jnp.float32
BF16 = jnp.bfloat16


def mod4(value):
    return lax.rem(value, RING)


def split(value):
    high = value.astype(BF16)
    return high, (value - high.astype(F32)).astype(BF16)


def dot(a, b):
    return jnp.dot(a, b, preferred_element_type=F32)


def dot_split(a, b):
    a_high, a_low = split(a)
    b_high, b_low = split(b)
    return dot(a_high, b_high) + (dot(a_high, b_low) + dot(a_low, b_high))


def main_kernel(
    w_hbm,
    sk_hbm,
    basis_out,
    coef_out,
    w_ref,
    sk_ref,
    own_sk,
    mate_sk,
    s_ref,
    part_f,
    part_b,
    img_in,
    img_mid,
    gram,
    total,
    gram_pair,
    gram_x,
    gram_y,
    gram_z,
    poly,
    basis,
    img,
    img_t,
    mate_send,
    mate_recv,
    z_f,
    z_b,
    z_in,
    row_f,
    row_b,
    col_in,
    coef,
    coef_mate,
    local_sem,
    send_sem,
    recv_sem,
):
    wide = lax.axis_index("wide")
    x = lax.axis_index("narrow")
    core = lax.rem(wide, 2)
    chip = wide // 2
    y, z = chip // RING, lax.rem(chip, RING)
    s1, s2 = 1 + 3 * core, 4 - 3 * core
    p1, p2 = z + core * (y - z), y + core * (z - y)
    mate = {"wide": chip * 2 + 1 - core}

    def chip_peer(a1, a2):
        return {"wide": (a1 * s1 + a2 * s2) * 2 + core}

    def y_peer(step):
        return {"wide": (mod4(y + step) * RING + z) * 2 + core}

    def z_peer(step):
        return {"wide": (y * RING + mod4(z + step)) * 2 + core}

    def x_peer(step):
        return {"narrow": mod4(x + step)}

    load_sk = pltpu.make_async_copy(sk_hbm, sk_ref, local_sem.at[1])
    load_sk.start()
    load_w = pltpu.make_async_copy(w_hbm, w_ref.at[pl.ds(0, ROWS)], local_sem.at[0])
    load_w.start()

    barrier = pltpu.get_barrier_semaphore()
    peers = [mate] + [f(s) for f in (x_peer, y_peer, z_peer) for s in (1, 2, 3)]
    for peer in peers:
        pl.semaphore_signal(barrier, inc=1, device_id=peer, device_id_type=MESH)
    load_sk.wait()
    own_sk[...] = sk_ref[...].astype(F32)
    w_ref[pl.ds(ROWS, PAD - ROWS), :] = jnp.zeros((PAD - ROWS, COLS), BF16)
    pl.semaphore_wait(barrier, len(peers))

    count = [0]
    pending = []

    def send(src, dst, peer):
        at = count[0]
        count[0] += 1
        copy = pltpu.make_async_remote_copy(
            src_ref=src,
            dst_ref=dst,
            send_sem=send_sem.at[at],
            recv_sem=recv_sem.at[at],
            device_id=peer,
            device_id_type=MESH,
        )
        copy.start()
        pending.append(copy)
        return copy

    def drain():
        for copy in pending:
            copy.wait_send()
        pending.clear()

    def gather16(blk, u, v, share, meanwhile):
        (pu, su), (pv, sv) = u, v

        def at_u(step):
            return {"wide": (mod4(pu + step) * su + pv * sv) * 2 + core}

        def at_v(step):
            return {"wide": (pu * su + mod4(pv + step) * sv) * 2 + core}

        own = blk(pu, pv)
        along_u = {s: send(own, own, at_u(s)) for s in (2, 1, 3)}
        along_v = [(pu, {s: send(own, own, at_v(s)) for s in (2, 1, 3)})]
        shared = [share(pu, pv)]
        for s in (1, 3, 2):
            along_u[s].wait_recv()
            a = mod4(pu + 4 - s)
            block = blk(a, pv)
            along_v.append((a, {t: send(block, block, at_v(t)) for t in (2, 1, 3)}))
            shared.append(share(a, pv))
        for a, copies in along_v:
            for t in (1, 3, 2):
                copies[t].wait_recv()
                shared.append(share(a, mod4(pv + 4 - t)))
        meanwhile()
        for copy in shared:
            copy.wait_recv()
        drain()

    axis1, axis2 = (p1, s1), (p2, s2)
    my_off = core * SKIP
    only_off = core * WIDE
    mate_off = (1 - core) * SKIP
    my_off2, mate_off2 = core * SKIP2, (1 - core) * SKIP2

    my_cols = pl.ds(pl.multiple_of(my_off, 128), WIDE)
    first = send(own_sk.at[:, pl.ds(pl.multiple_of(mate_off, 128), WIDE)], mate_sk, mate)
    first.wait_recv()
    mine, other = own_sk[:, my_cols], mate_sk[...]
    even = core == 0
    pair = jnp.concatenate([jnp.where(even, mine, other), jnp.where(even, other, mine)], axis=0)
    s_ref[pl.ds(pl.multiple_of(chip * BLK, BLK), BLK), my_cols] = pair.astype(BF16)

    def sketch_block(a1, a2):
        return s_ref.at[pl.ds(pl.multiple_of((a1 * s1 + a2 * s2) * BLK, BLK), BLK), my_cols]

    def share_sketch(a1, a2):
        rows = pl.ds(pl.multiple_of((a1 * s1 + a2 * s2) * BLK, BLK), BLK)
        block = s_ref.at[rows, pl.ds(pl.multiple_of(only_off, 128), SKIP)]
        return send(block, block, mate)

    def rows_dot(rows, off, start, width):
        return lax.dot_general(
            w_ref[rows, pl.ds(pl.multiple_of(off + start, 128), width)],
            s_ref[:, pl.ds(pl.multiple_of(off + start, 128), width)],
            (((1,), (1,)), ((), ())),
            preferred_element_type=F32,
        )

    def own_columns():
        load_w.wait()
        part_f[...] = rows_dot(pl.ds(0, PAD), my_off, 0, WIDE)

    gather16(sketch_block, axis1, axis2, share_sketch, own_columns)
    mate_only = (1 - core) * WIDE

    def piece(step, start, size):
        return pl.ds(pl.multiple_of(mod4(x + step) * CHUNK + start, 16), size)

    def add_columns(step, start, size):
        rows = piece(step, start, size)
        value = part_f[rows, :] + rows_dot(rows, mate_only, 0, SKIP)
        part_f[rows, :] = value
        part_b[rows, :] = value.astype(BF16)

    phase = []
    for start, size in STREAMS:
        for step in (2, 1, 3):
            add_columns(step, start, size)
            half = size // 2
            a, b = piece(step, start, half), piece(step, start + half, half)
            if step == 2:
                n = len(phase)
                one = {"a": lambda k, n=n, half=half: img_in.at[n, k, pl.ds(0, half)], "half": half, "start": start}
                phase.append(one)
                one[0] = send(part_b.at[a], one["a"](0), x_peer(1))
                one[1] = send(part_b.at[b], one["a"](1), x_peer(3))
            elif step == 1:
                one[2] = send(part_b.at[b], one["a"](2), x_peer(1))
            else:
                one[3] = send(part_b.at[a], one["a"](3), x_peer(3))
    for start, size in STREAMS:
        add_columns(0, start, size)

    def inbox(one, n, k):
        return img_in[n, k, pl.ds(0, one["half"]), :].astype(F32)

    for n, one in enumerate(phase):
        start, half = one["start"], one["half"]
        middle = pl.ds(0, half)
        one[0].wait_recv()
        img_mid[n, 0, middle, :] = (part_f[piece(1, start, half), :] + inbox(one, n, 0)).astype(BF16)
        one[4] = send(img_mid.at[n, 0, middle], one["a"](4), x_peer(1))
        one[1].wait_recv()
        img_mid[n, 1, middle, :] = (part_f[piece(3, start + half, half), :] + inbox(one, n, 1)).astype(BF16)
        one[5] = send(img_mid.at[n, 1, middle], one["a"](5), x_peer(3))

    for n, one in enumerate(phase):
        start, half = one["start"], one["half"]
        own_a, own_b = piece(0, start, half), piece(0, start + half, half)
        one[3].wait_recv()
        one[4].wait_recv()
        img[own_a, :] = (part_f[own_a, :] + inbox(one, n, 3) + inbox(one, n, 4)).astype(BF16)
        one["a_right"] = send(img.at[own_a], img.at[own_a], x_peer(1))
        one[2].wait_recv()
        one[5].wait_recv()
        img[own_b, :] = (part_f[own_b, :] + inbox(one, n, 2) + inbox(one, n, 5)).astype(BF16)
        one["b_left"] = send(img.at[own_b], img.at[own_b], x_peer(3))
        one["b_right"] = send(img.at[own_b], img.at[own_b], x_peer(1))
        one["a_left"] = send(img.at[own_a], img.at[own_a], x_peer(3))

    def pass_on(one):
        start, half = one["start"], one["half"]
        one["a_right"].wait_recv()
        rows = piece(3, start, half)
        one["opp_a"] = send(img.at[rows], img.at[rows], x_peer(1))
        one["b_left"].wait_recv()
        rows = piece(1, start + half, half)
        one["opp_b"] = send(img.at[rows], img.at[rows], x_peer(3))

    own = img[piece(0, 0, CHUNK), :]
    gram[...] = lax.dot_general(own, own, (((0,), (0,)), ((), ())), preferred_element_type=F32)
    g_core = pl.multiple_of(core * 128, 128)
    g_mate = pl.multiple_of((1 - core) * 128, 128)
    copy = send(gram.at[pl.ds(g_mate, 128)], gram_pair, mate)
    for one in phase[:-1]:
        pass_on(one)
    copy.wait_recv()
    gram[pl.ds(g_core, 128), :] = gram[pl.ds(g_core, 128), :] + gram_pair[...]

    def gram_rows(ax):
        return pl.ds(pl.multiple_of(core * 128 + ax * 32, 32), 32)

    at_x = gram_rows(x)
    gram_stage = {s: send(gram.at[gram_rows(mod4(x + s))], gram_x.at[s - 1], x_peer(s)) for s in (2, 1, 3)}
    pass_on(phase[-1])
    for copy in gram_stage.values():
        copy.wait_recv()
    gram_z[0] = gram[at_x, :] + gram_x[0] + gram_x[1] + gram_x[2]
    gram_stage = [send(gram_z.at[0], gram_z.at[s], z_peer(s)) for s in (2, 1, 3)]
    for one in phase:
        for name in ("a_left", "b_right", "opp_a", "opp_b"):
            one[name].wait_recv()

    img_t[...] = img[...].T

    def partial(off, part):
        cols = pl.ds(pl.multiple_of(off + part * PART, 128), PART)
        return dot(img_t[...], w_ref[:, cols])

    copies = []
    for part in (0, 1):
        mate_send[part] = partial(mate_off2, part).astype(BF16)
        copies.append(send(mate_send.at[part], mate_recv.at[part], mate))
    for part in (0, 1):
        value = partial(my_off2, part)
        copies[part].wait_recv()
        value = value + mate_recv[part].astype(F32)
        for tile in range(PART // 128):
            block = value[:, tile * 128 : tile * 128 + 128]
            z_f[part * (PART // 128) + tile] = block
            z_b[part * (PART // 128) + tile] = block.astype(BF16)

    for copy in gram_stage:
        copy.wait_recv()
    gram_y[0] = gram_z[0] + gram_z[1] + gram_z[2] + gram_z[3]
    gram_stage = [send(gram_y.at[0], gram_y.at[s], y_peer(s)) for s in (2, 1, 3)]

    scatter = {}
    for s in (2, 1, 3):
        a1 = mod4(p1 + s)
        for a2 in range(RING):
            scatter[s, a2] = send(z_b.at[a1 * s1 + a2 * s2], z_in.at[s - 1, a2], chip_peer(a1, p2))
    for copy in gram_stage:
        copy.wait_recv()
    total[at_x, :] = gram_y[0] + gram_y[1] + gram_y[2] + gram_y[3]
    gram_stage = [send(total.at[at_x], total.at[at_x], x_peer(s)) for s in (2, 1, 3)]
    for copy in gram_stage:
        copy.wait_recv()
    rows = pl.ds(g_core, 128)
    copy = send(total.at[rows], total.at[rows], mate)
    copy.wait_recv()

    def row_sum(a2):
        for s in (1, 2, 3):
            scatter[s, a2].wait_recv()

    for a2 in range(RING):
        row_sum(a2)
        value = z_f[p1 * s1 + a2 * s2]
        for s in (1, 2, 3):
            value = value + z_in[s - 1, a2].astype(F32)
        row_f[a2] = value
        row_b[a2] = value.astype(BF16)
    column = [
        send(row_b.at[mod4(p2 + s)], col_in.at[s - 1], chip_peer(p1, mod4(p2 + s))) for s in (2, 1, 3)
    ]

    whole = total[...]
    diagonal = lax.broadcasted_iota(jnp.int32, (RANK, RANK), 0) == lax.broadcasted_iota(
        jnp.int32, (RANK, RANK), 1
    )
    trace = jnp.sum(jnp.where(diagonal, whole, 0.0), keepdims=True)
    poly[pl.ds(0, RANK), :] = whole / trace
    poly[pl.ds(RANK, RANK), :] = jnp.where(diagonal, 1.0 / jnp.sqrt(trace), 0.0)

    def factor(g):
        return jnp.where(diagonal, 1.5, 0.0) - 0.5 * g

    def iteration(_, carry):
        both = poly[...]
        p = factor(both[:RANK])
        p_high, p_low = split(p)

        def times_p(a):
            a_high, a_low = split(a)
            return dot(a_high, p_high) + (dot(a_high, p_low) + dot(a_low, p_high))

        both = times_p(both)
        poly[pl.ds(RANK, RANK), :] = both[RANK:]
        poly[pl.ds(0, RANK), :] = times_p(both[:RANK])
        return carry

    lax.fori_loop(0, ITERS - 1, iteration, 0)
    q = dot_split(poly[pl.ds(RANK, RANK), :], factor(poly[pl.ds(0, RANK), :]))
    for copy in column:
        copy.wait_recv()
    mine = row_f[p2]
    for s in range(3):
        mine = mine + col_in[s].astype(F32)
    coef[chip] = dot_split(q, mine).astype(BF16)

    q_high, q_low = split(q)

    def coef_block(a2, a1):
        return coef.at[a1 * s1 + a2 * s2]

    def share_coef(a2, a1):
        at = a1 * s1 + a2 * s2
        return send(coef.at[at], coef_mate.at[at], mate)

    def basis_rows():
        basis[...] = (dot(img[...], q_high) + dot(img[...], q_low)).astype(BF16)
        save = pltpu.make_async_copy(basis.at[pl.ds(0, ROWS)], basis_out, local_sem.at[1])
        save.start()
        return save

    saved = []
    gather16(coef_block, axis2, axis1, share_coef, lambda: saved.append(basis_rows()))
    save_basis = saved[0]
    save_own = pltpu.make_async_copy(coef, coef_out.at[core], local_sem.at[2])
    save_mate = pltpu.make_async_copy(coef_mate, coef_out.at[1 - core], local_sem.at[3])
    save_own.start()
    save_mate.start()
    save_basis.wait()
    save_own.wait()
    save_mate.wait()
    assert count[0] <= COPIES, count[0]


COPIES = 160
STEP = 240


def residual_kernel(w_ref, basis_ref, coef_ref, residual_out, own_ref, whole, result, sem):
    for tile in range(COLS // 128):
        at = (0, tile) if tile < TILES else (1, tile - SKIP2 // 128)
        whole[:, tile * 128 : tile * 128 + 128] = coef_ref[at]
    copies = []
    for start in range(0, ROWS, STEP):
        rows = pl.ds(start, min(STEP, ROWS - start))
        left = basis_ref[rows, :]
        for column in range(0, COLS, RANK):
            cols = pl.ds(column, min(RANK, COLS - column))
            value = w_ref[rows, cols].astype(F32) - dot(left, whole[:, cols])
            result[rows, cols] = value.astype(BF16)
        copy = pltpu.make_async_copy(result.at[rows], residual_out.at[rows], sem.at[len(copies)])
        copy.start()
        copies.append(copy)
    wide = lax.axis_index("wide")
    block = whole[pl.ds(pl.multiple_of((wide // 2) * BLK, BLK), BLK), :].astype(F32)
    first = lax.rem(wide, 2) == 0
    own_ref[...] = jnp.where(first, block[:8], block[8:]).astype(BF16)
    for copy in copies:
        copy.wait()


def shards(weight, sketch):
    basis, coef = pl.pallas_call(
        main_kernel,
        out_shape=(
            jax.ShapeDtypeStruct((ROWS, RANK), BF16),
            jax.ShapeDtypeStruct((2, TILES, RANK, 128), BF16),
        ),
        in_specs=[pl.BlockSpec(memory_space=pltpu.HBM)] * 2,
        out_specs=[pl.BlockSpec(memory_space=pl.ANY)] * 2,
        scratch_shapes=[
            pltpu.VMEM((PAD, COLS), BF16),
            pltpu.VMEM((8, COLS), BF16),
            pltpu.VMEM((8, COLS), F32),
            pltpu.VMEM((8, WIDE), F32),
            pltpu.VMEM((RANK, COLS), BF16),
            pltpu.VMEM((PAD, RANK), F32),
            pltpu.VMEM((PAD, RANK), BF16),
            pltpu.VMEM((len(STREAMS), 6, 96, RANK), BF16),
            pltpu.VMEM((len(STREAMS), 2, 96, RANK), BF16),
            pltpu.VMEM((RANK, RANK), F32),
            pltpu.VMEM((RANK, RANK), F32),
            pltpu.VMEM((128, RANK), F32),
            pltpu.VMEM((3, 32, RANK), F32),
            pltpu.VMEM((4, 32, RANK), F32),
            pltpu.VMEM((4, 32, RANK), F32),
            pltpu.VMEM((2 * RANK, RANK), F32),
            pltpu.VMEM((PAD, RANK), BF16),
            pltpu.VMEM((PAD, RANK), BF16),
            pltpu.VMEM((RANK, PAD), BF16),
            pltpu.VMEM((2, RANK, PART), BF16),
            pltpu.VMEM((2, RANK, PART), BF16),
            pltpu.VMEM((TILES, RANK, 128), F32),
            pltpu.VMEM((TILES, RANK, 128), BF16),
            pltpu.VMEM((3, RING, RANK, 128), BF16),
            pltpu.VMEM((RING, RANK, 128), F32),
            pltpu.VMEM((RING, RANK, 128), BF16),
            pltpu.VMEM((3, RANK, 128), BF16),
            pltpu.VMEM((TILES, RANK, 128), BF16),
            pltpu.VMEM((TILES, RANK, 128), BF16),
            pltpu.SemaphoreType.DMA((4,)),
            pltpu.SemaphoreType.DMA((COPIES,)),
            pltpu.SemaphoreType.DMA((COPIES,)),
        ],
        compiler_params=pltpu.CompilerParams(
            collective_id=0, has_side_effects=True, vmem_limit_bytes=44 * 1024 * 1024
        ),
        cost_estimate=pl.CostEstimate(
            flops=2 * 2 * ROWS * COLS * RANK, bytes_accessed=2 * ROWS * COLS, transcendentals=0
        ),
        name="polar_basis",
    )(weight, sketch.T)

    residual, own = pl.pallas_call(
        residual_kernel,
        out_shape=(
            jax.ShapeDtypeStruct((ROWS, COLS), BF16),
            jax.ShapeDtypeStruct((8, COLS), BF16),
        ),
        in_specs=[pl.BlockSpec(memory_space=pltpu.VMEM)] * 3,
        out_specs=[
            pl.BlockSpec(memory_space=pl.ANY),
            pl.BlockSpec(memory_space=pltpu.VMEM),
        ],
        scratch_shapes=[
            pltpu.VMEM((RANK, COLS), BF16),
            pltpu.VMEM((ROWS, COLS), BF16),
            pltpu.SemaphoreType.DMA((pl.cdiv(ROWS, STEP),)),
        ],
        compiler_params=pltpu.CompilerParams(vmem_limit_bytes=24 * 1024 * 1024),
        cost_estimate=pl.CostEstimate(
            flops=2 * ROWS * COLS * RANK, bytes_accessed=4 * ROWS * COLS, transcendentals=0
        ),
        name="residual",
    )(weight, basis, coef)
    return own, residual


def solution(mesh):
    placed = (P("wide", "narrow"), P("narrow", "wide"))
    return jax.shard_map(
        shards,
        mesh=mesh,
        in_specs=placed,
        out_specs=(P("wide", "narrow"), P("wide", "narrow")),
        check_vma=False,
    )
```

```python
import jax
import jax.numpy as jnp
from jax import lax
from jax.experimental import pallas as pl
from jax.experimental.pallas import tpu as pltpu
from jax.sharding import PartitionSpec as P

ITERS = 6
RING = 4
RANK = 256
ROWS = 1392
COLS = 3712
PAD = 1408
CHUNK = PAD // RING
STREAMS = ((0, 192), (192, 160))
BLK = 16
WIDE = 1920
SKIP = COLS - WIDE
TILES = 16
SKIP2 = COLS - TILES * 128
MESH = pl.DeviceIdType.MESH
F32 = jnp.float32
BF16 = jnp.bfloat16


def mod4(value):
    return lax.rem(value, RING)


def split(value):
    high = value.astype(BF16)
    return high, (value - high.astype(F32)).astype(BF16)


def dot(a, b):
    return jnp.dot(a, b, preferred_element_type=F32)


def dot_split(a, b):
    a_high, a_low = split(a)
    b_high, b_low = split(b)
    return dot(a_high, b_high) + (dot(a_high, b_low) + dot(a_low, b_high))


def main_kernel(
    w_hbm,
    sk_hbm,
    basis_out,
    coef_out,
    w_ref,
    sk_ref,
    own_sk,
    mate_sk,
    s_ref,
    part_f,
    part_b,
    img_in,
    img_mid,
    gram,
    total,
    gram_pair,
    gram_x,
    gram_y,
    gram_z,
    poly,
    img,
    img_t,
    mate_send,
    mate_recv,
    z_f,
    z_b,
    z_in,
    row_f,
    row_b,
    col_in,
    local_sem,
    send_sem,
    recv_sem,
):
    wide = lax.axis_index("wide")
    x = lax.axis_index("narrow")
    core = lax.rem(wide, 2)
    chip = wide // 2
    y, z = chip // RING, lax.rem(chip, RING)
    s1, s2 = 1 + 3 * core, 4 - 3 * core
    p1, p2 = z + core * (y - z), y + core * (z - y)
    mate = {"wide": chip * 2 + 1 - core}

    def chip_peer(a1, a2):
        return {"wide": (a1 * s1 + a2 * s2) * 2 + core}

    def y_peer(step):
        return {"wide": (mod4(y + step) * RING + z) * 2 + core}

    def z_peer(step):
        return {"wide": (y * RING + mod4(z + step)) * 2 + core}

    def x_peer(step):
        return {"narrow": mod4(x + step)}

    load_sk = pltpu.make_async_copy(sk_hbm, sk_ref, local_sem.at[1])
    load_sk.start()
    load_w = pltpu.make_async_copy(w_hbm, w_ref.at[pl.ds(0, ROWS)], local_sem.at[0])
    load_w.start()

    barrier = pltpu.get_barrier_semaphore()
    peers = [mate] + [f(s) for f in (x_peer, y_peer, z_peer) for s in (1, 2, 3)]
    for peer in peers:
        pl.semaphore_signal(barrier, inc=1, device_id=peer, device_id_type=MESH)
    load_sk.wait()
    own_sk[...] = sk_ref[...].astype(F32)
    w_ref[pl.ds(ROWS, PAD - ROWS), :] = jnp.zeros((PAD - ROWS, COLS), BF16)
    pl.semaphore_wait(barrier, len(peers))

    count = [0]
    pending = []

    def send(src, dst, peer):
        at = count[0]
        count[0] += 1
        copy = pltpu.make_async_remote_copy(
            src_ref=src,
            dst_ref=dst,
            send_sem=send_sem.at[at],
            recv_sem=recv_sem.at[at],
            device_id=peer,
            device_id_type=MESH,
        )
        copy.start()
        pending.append(copy)
        return copy

    def drain():
        for copy in pending:
            copy.wait_send()
        pending.clear()

    def gather16(blk, u, v, share, meanwhile):
        (pu, su), (pv, sv) = u, v

        def at_u(step):
            return {"wide": (mod4(pu + step) * su + pv * sv) * 2 + core}

        def at_v(step):
            return {"wide": (pu * su + mod4(pv + step) * sv) * 2 + core}

        own = blk(pu, pv)
        along_u = {s: send(own, own, at_u(s)) for s in (2, 1, 3)}
        along_v = [(pu, {s: send(own, own, at_v(s)) for s in (2, 1, 3)})]
        shared = [share(pu, pv)]
        for s in (1, 3, 2):
            along_u[s].wait_recv()
            a = mod4(pu + 4 - s)
            block = blk(a, pv)
            along_v.append((a, {t: send(block, block, at_v(t)) for t in (2, 1, 3)}))
            shared.append(share(a, pv))
        for a, copies in along_v:
            for t in (1, 3, 2):
                copies[t].wait_recv()
                shared.append(share(a, mod4(pv + 4 - t)))
        meanwhile()
        for copy in shared:
            copy.wait_recv()
        drain()

    axis1, axis2 = (p1, s1), (p2, s2)
    my_off = core * SKIP
    only_off = core * WIDE
    mate_off = (1 - core) * SKIP
    my_off2, mate_off2 = core * SKIP2, (1 - core) * SKIP2

    my_cols = pl.ds(pl.multiple_of(my_off, 128), WIDE)
    first = send(own_sk.at[:, pl.ds(pl.multiple_of(mate_off, 128), WIDE)], mate_sk, mate)
    first.wait_recv()
    mine, other = own_sk[:, my_cols], mate_sk[...]
    even = core == 0
    pair = jnp.concatenate([jnp.where(even, mine, other), jnp.where(even, other, mine)], axis=0)
    s_ref[pl.ds(pl.multiple_of(chip * BLK, BLK), BLK), my_cols] = pair.astype(BF16)

    def sketch_block(a1, a2):
        return s_ref.at[pl.ds(pl.multiple_of((a1 * s1 + a2 * s2) * BLK, BLK), BLK), my_cols]

    def share_sketch(a1, a2):
        rows = pl.ds(pl.multiple_of((a1 * s1 + a2 * s2) * BLK, BLK), BLK)
        block = s_ref.at[rows, pl.ds(pl.multiple_of(only_off, 128), SKIP)]
        return send(block, block, mate)

    def rows_dot(rows, off, start, width):
        return lax.dot_general(
            w_ref[rows, pl.ds(pl.multiple_of(off + start, 128), width)],
            s_ref[:, pl.ds(pl.multiple_of(off + start, 128), width)],
            (((1,), (1,)), ((), ())),
            preferred_element_type=F32,
        )

    def own_columns():
        load_w.wait()
        part_f[...] = rows_dot(pl.ds(0, PAD), my_off, 0, WIDE)

    gather16(sketch_block, axis1, axis2, share_sketch, own_columns)
    mate_only = (1 - core) * WIDE

    def piece(step, start, size):
        return pl.ds(pl.multiple_of(mod4(x + step) * CHUNK + start, 16), size)

    def add_columns(step, start, size):
        rows = piece(step, start, size)
        value = part_f[rows, :] + rows_dot(rows, mate_only, 0, SKIP)
        part_f[rows, :] = value
        part_b[rows, :] = value.astype(BF16)

    phase = []
    for n, (start, size) in enumerate(STREAMS):
        half = size // 2
        one = {"start": start, "half": half}
        one["in"] = [img_in.at[n, k, pl.ds(0, half)] for k in range(6)]
        phase.append(one)
        add_columns(2, start, size)
        one[0] = send(part_b.at[piece(2, start, half)], one["in"][0], x_peer(1))
        one[1] = send(part_b.at[piece(2, start + half, half)], one["in"][1], x_peer(3))
    for one, (start, size) in zip(phase, STREAMS):
        half = size // 2
        add_columns(1, start, size)
        one[2] = send(part_b.at[piece(1, start + half, half)], one["in"][2], x_peer(1))
        add_columns(3, start, size)
        one[3] = send(part_b.at[piece(3, start, half)], one["in"][3], x_peer(3))
    for start, size in STREAMS:
        add_columns(0, start, size)

    def inbox(one, n, k):
        return img_in[n, k, pl.ds(0, one["half"]), :].astype(F32)

    for n, one in enumerate(phase):
        start, half = one["start"], one["half"]
        middle = pl.ds(0, half)
        one[0].wait_recv()
        img_mid[n, 0, middle, :] = (part_f[piece(1, start, half), :] + inbox(one, n, 0)).astype(BF16)
        one[4] = send(img_mid.at[n, 0, middle], one["in"][4], x_peer(1))
        one[1].wait_recv()
        img_mid[n, 1, middle, :] = (part_f[piece(3, start + half, half), :] + inbox(one, n, 1)).astype(BF16)
        one[5] = send(img_mid.at[n, 1, middle], one["in"][5], x_peer(3))

    for n, one in enumerate(phase):
        start, half = one["start"], one["half"]
        own_a, own_b = piece(0, start, half), piece(0, start + half, half)
        one[3].wait_recv()
        one[4].wait_recv()
        img[own_a, :] = (part_f[own_a, :] + inbox(one, n, 3) + inbox(one, n, 4)).astype(BF16)
        one["a_right"] = send(img.at[own_a], img.at[own_a], x_peer(1))
        one[2].wait_recv()
        one[5].wait_recv()
        img[own_b, :] = (part_f[own_b, :] + inbox(one, n, 2) + inbox(one, n, 5)).astype(BF16)
        one["b_left"] = send(img.at[own_b], img.at[own_b], x_peer(3))
        one["b_right"] = send(img.at[own_b], img.at[own_b], x_peer(1))
        one["a_left"] = send(img.at[own_a], img.at[own_a], x_peer(3))

    def pass_on(one):
        start, half = one["start"], one["half"]
        one["a_right"].wait_recv()
        rows = piece(3, start, half)
        one["opp_a"] = send(img.at[rows], img.at[rows], x_peer(1))
        one["b_left"].wait_recv()
        rows = piece(1, start + half, half)
        one["opp_b"] = send(img.at[rows], img.at[rows], x_peer(3))

    own = img[piece(0, 0, CHUNK), :]
    gram[...] = lax.dot_general(own, own, (((0,), (0,)), ((), ())), preferred_element_type=F32)
    g_core = pl.multiple_of(core * 128, 128)
    g_mate = pl.multiple_of((1 - core) * 128, 128)
    copy = send(gram.at[pl.ds(g_mate, 128)], gram_pair, mate)
    for one in phase[:-1]:
        pass_on(one)
    copy.wait_recv()
    gram[pl.ds(g_core, 128), :] = gram[pl.ds(g_core, 128), :] + gram_pair[...]

    def gram_rows(ax):
        return pl.ds(pl.multiple_of(core * 128 + ax * 32, 32), 32)

    at_x = gram_rows(x)
    gram_stage = {s: send(gram.at[gram_rows(mod4(x + s))], gram_x.at[s - 1], x_peer(s)) for s in (2, 1, 3)}
    pass_on(phase[-1])
    for copy in gram_stage.values():
        copy.wait_recv()
    gram_z[0] = gram[at_x, :] + gram_x[0] + gram_x[1] + gram_x[2]
    gram_stage = [send(gram_z.at[0], gram_z.at[s], z_peer(s)) for s in (2, 1, 3)]
    for one in phase:
        for name in ("a_left", "b_right", "opp_a", "opp_b"):
            one[name].wait_recv()

    img_t[...] = img[...].T

    def group(off, a2, sa, sb):
        columns = [
            w_ref[:, pl.ds(pl.multiple_of(off + (a1 * sa + a2 * sb) * 128, 128), 128)]
            for a1 in range(RING)
        ]
        return dot(img_t[...], jnp.concatenate(columns, axis=1))

    turns = (2, 1, 3, 0)
    copies = []
    for j, s in enumerate(turns):
        mate_send[j] = group(mate_off2, mod4(p1 + s), s2, s1).astype(BF16)
        copies.append(send(mate_send.at[j], mate_recv.at[j], mate))

    scatter = []
    for j, s in enumerate(turns):
        value = group(my_off2, mod4(p2 + s), s1, s2)
        copies[j].wait_recv()
        value = value + mate_recv[j].astype(F32)
        for a1 in range(RING):
            block = value[:, a1 * 128 : a1 * 128 + 128]
            z_f[j, a1] = block
            z_b[j, a1] = block.astype(BF16)
        if j == 0:
            for copy in gram_stage:
                copy.wait_recv()
            gram_y[0] = gram_z[0] + gram_z[1] + gram_z[2] + gram_z[3]
            gram_stage = [send(gram_y.at[0], gram_y.at[t], y_peer(t)) for t in (2, 1, 3)]
        peers_u = [(t, mod4(p1 + t)) for t in (2, 1, 3)]
        scatter.append([send(z_b.at[j, a1], z_in.at[j, t - 1], chip_peer(a1, p2)) for t, a1 in peers_u])

    def row_sum(j):
        for copy in scatter[j]:
            copy.wait_recv()
        value = z_f[j, p1]
        for t in range(3):
            value = value + z_in[j, t].astype(F32)
        return value

    def send_row(j):
        s = turns[j]
        row_b[j] = row_sum(j).astype(BF16)
        return send(row_b.at[j], col_in.at[s - 1], chip_peer(p1, mod4(p2 + s)))

    for copy in gram_stage:
        copy.wait_recv()
    total[at_x, :] = gram_y[0] + gram_y[1] + gram_y[2] + gram_y[3]
    gram_stage = [send(total.at[at_x], total.at[at_x], x_peer(s)) for s in (2, 1, 3)]
    column = [send_row(0), send_row(1)]
    for copy in gram_stage:
        copy.wait_recv()
    rows = pl.ds(g_core, 128)
    copy = send(total.at[rows], total.at[rows], mate)
    column.append(send_row(2))
    row_f[...] = row_sum(3)
    copy.wait_recv()

    whole = total[...]
    diagonal = lax.broadcasted_iota(jnp.int32, (RANK, RANK), 0) == lax.broadcasted_iota(
        jnp.int32, (RANK, RANK), 1
    )
    trace = jnp.sum(jnp.where(diagonal, whole, 0.0), keepdims=True)
    poly[pl.ds(0, RANK), :] = whole / trace
    poly[pl.ds(RANK, RANK), :] = jnp.where(diagonal, 1.0 / jnp.sqrt(trace), 0.0)

    def factor(g):
        return jnp.where(diagonal, 1.5, 0.0) - 0.5 * g

    def iteration(_, carry):
        both = poly[...]
        p = factor(both[:RANK])
        p_high, p_low = split(p)

        def times_p(a):
            a_high, a_low = split(a)
            return dot(a_high, p_high) + (dot(a_high, p_low) + dot(a_low, p_high))

        both = times_p(both)
        poly[pl.ds(RANK, RANK), :] = both[RANK:]
        poly[pl.ds(0, RANK), :] = times_p(both[:RANK])
        return carry

    lax.fori_loop(0, ITERS - 1, iteration, 0)
    q = dot_split(poly[pl.ds(RANK, RANK), :], factor(poly[pl.ds(0, RANK), :]))
    for copy in column:
        copy.wait_recv()
    mine = row_f[...]
    for s in range(3):
        mine = mine + col_in[s].astype(F32)
    coef_out[core, chip] = dot_split(q, mine).astype(BF16)

    q_high, q_low = split(q)

    def coef_block(a2, a1):
        return coef_out.at[core, a1 * s1 + a2 * s2]

    def share_coef(a2, a1):
        return send(coef_block(a2, a1), coef_block(a2, a1), mate)

    def basis_rows():
        own = img[pl.ds(0, ROWS), :]
        basis_out[...] = (dot(own, q_high) + dot(own, q_low)).astype(BF16)

    gather16(coef_block, axis2, axis1, share_coef, basis_rows)
    assert count[0] <= COPIES, count[0]


COPIES = 160
STEP = 240


def residual_kernel(w_ref, basis_ref, coef_ref, residual_out, own_ref, whole, result, sem):
    for tile in range(COLS // 128):
        at = (0, tile) if tile < TILES else (1, tile - SKIP2 // 128)
        whole[:, tile * 128 : tile * 128 + 128] = coef_ref[at]
    copies = []
    for start in range(0, ROWS, STEP):
        rows = pl.ds(start, min(STEP, ROWS - start))
        left = basis_ref[rows, :]
        for column in range(0, COLS, RANK):
            cols = pl.ds(column, min(RANK, COLS - column))
            value = w_ref[rows, cols].astype(F32) - dot(left, whole[:, cols])
            result[rows, cols] = value.astype(BF16)
        copy = pltpu.make_async_copy(result.at[rows], residual_out.at[rows], sem.at[len(copies)])
        copy.start()
        copies.append(copy)
    wide = lax.axis_index("wide")
    block = whole[pl.ds(pl.multiple_of((wide // 2) * BLK, BLK), BLK), :].astype(F32)
    first = lax.rem(wide, 2) == 0
    own_ref[...] = jnp.where(first, block[:8], block[8:]).astype(BF16)
    for copy in copies:
        copy.wait()


def shards(weight, sketch):
    basis, coef = pl.pallas_call(
        main_kernel,
        out_shape=(
            jax.ShapeDtypeStruct((ROWS, RANK), BF16),
            jax.ShapeDtypeStruct((2, TILES, RANK, 128), BF16),
        ),
        in_specs=[pl.BlockSpec(memory_space=pltpu.HBM)] * 2,
        out_specs=[pl.BlockSpec(memory_space=pltpu.VMEM)] * 2,
        scratch_shapes=[
            pltpu.VMEM((PAD, COLS), BF16),
            pltpu.VMEM((8, COLS), BF16),
            pltpu.VMEM((8, COLS), F32),
            pltpu.VMEM((8, WIDE), F32),
            pltpu.VMEM((RANK, COLS), BF16),
            pltpu.VMEM((PAD, RANK), F32),
            pltpu.VMEM((PAD, RANK), BF16),
            pltpu.VMEM((len(STREAMS), 6, 96, RANK), BF16),
            pltpu.VMEM((len(STREAMS), 2, 96, RANK), BF16),
            pltpu.VMEM((RANK, RANK), F32),
            pltpu.VMEM((RANK, RANK), F32),
            pltpu.VMEM((128, RANK), F32),
            pltpu.VMEM((3, 32, RANK), F32),
            pltpu.VMEM((4, 32, RANK), F32),
            pltpu.VMEM((4, 32, RANK), F32),
            pltpu.VMEM((2 * RANK, RANK), F32),
            pltpu.VMEM((PAD, RANK), BF16),
            pltpu.VMEM((RANK, PAD), BF16),
            pltpu.VMEM((RING, RANK, 512), BF16),
            pltpu.VMEM((RING, RANK, 512), BF16),
            pltpu.VMEM((RING, RING, RANK, 128), F32),
            pltpu.VMEM((RING, RING, RANK, 128), BF16),
            pltpu.VMEM((RING, 3, RANK, 128), BF16),
            pltpu.VMEM((RANK, 128), F32),
            pltpu.VMEM((3, RANK, 128), BF16),
            pltpu.VMEM((3, RANK, 128), BF16),
            pltpu.SemaphoreType.DMA((2,)),
            pltpu.SemaphoreType.DMA((COPIES,)),
            pltpu.SemaphoreType.DMA((COPIES,)),
        ],
        compiler_params=pltpu.CompilerParams(
            collective_id=0, has_side_effects=True, vmem_limit_bytes=44 * 1024 * 1024
        ),
        cost_estimate=pl.CostEstimate(
            flops=2 * 2 * ROWS * COLS * RANK, bytes_accessed=2 * ROWS * COLS, transcendentals=0
        ),
        name="polar_basis",
    )(weight, sketch.T)

    residual, own = pl.pallas_call(
        residual_kernel,
        out_shape=(
            jax.ShapeDtypeStruct((ROWS, COLS), BF16),
            jax.ShapeDtypeStruct((8, COLS), BF16),
        ),
        in_specs=[pl.BlockSpec(memory_space=pltpu.VMEM)] * 3,
        out_specs=[
            pl.BlockSpec(memory_space=pl.ANY),
            pl.BlockSpec(memory_space=pltpu.VMEM),
        ],
        scratch_shapes=[
            pltpu.VMEM((RANK, COLS), BF16),
            pltpu.VMEM((ROWS, COLS), BF16),
            pltpu.SemaphoreType.DMA((pl.cdiv(ROWS, STEP),)),
        ],
        compiler_params=pltpu.CompilerParams(vmem_limit_bytes=24 * 1024 * 1024),
        cost_estimate=pl.CostEstimate(
            flops=2 * ROWS * COLS * RANK, bytes_accessed=4 * ROWS * COLS, transcendentals=0
        ),
        name="residual",
    )(weight, basis, coef)
    return own, residual


def solution(mesh):
    placed = (P("wide", "narrow"), P("narrow", "wide"))
    return jax.shard_map(
        shards,
        mesh=mesh,
        in_specs=placed,
        out_specs=(P("wide", "narrow"), P("wide", "narrow")),
        check_vma=False,
    )
```

```python
import jax
import jax.numpy as jnp
from jax import lax
from jax.experimental import pallas as pl
from jax.experimental.pallas import tpu as pltpu
from jax.sharding import PartitionSpec as P

ITERS = 6
RING = 4
RANK = 256
ROWS = 1392
COLS = 3712
PAD = 1408
CHUNK = PAD // RING
STREAMS = ((0, 192), (192, 160))
BLK = 16
WIDE = 1920
SKIP = COLS - WIDE
TILES = 16
SKIP2 = COLS - TILES * 128
MESH = pl.DeviceIdType.MESH
F32 = jnp.float32
BF16 = jnp.bfloat16


def mod4(value):
    return lax.rem(value, RING)


def split(value):
    high = value.astype(BF16)
    return high, (value - high.astype(F32)).astype(BF16)


def dot(a, b):
    return jnp.dot(a, b, preferred_element_type=F32)


def dot_split(a, b):
    a_high, a_low = split(a)
    b_high, b_low = split(b)
    return dot(a_high, b_high) + (dot(a_high, b_low) + dot(a_low, b_high))


def main_kernel(
    w_hbm,
    sk_hbm,
    basis_out,
    coef_out,
    w_ref,
    sk_ref,
    own_sk,
    mate_sk,
    s_ref,
    part_f,
    part_b,
    img_in,
    img_mid,
    gram,
    gram_own,
    total,
    gram_pair,
    gram_x,
    gram_y,
    gram_z,
    poly,
    img,
    img_t,
    mate_send,
    mate_recv,
    z_f,
    z_b,
    z_in,
    row_f,
    row_b,
    col_in,
    local_sem,
    send_sem,
    recv_sem,
):
    wide = lax.axis_index("wide")
    x = lax.axis_index("narrow")
    core = lax.rem(wide, 2)
    chip = wide // 2
    y, z = chip // RING, lax.rem(chip, RING)
    s1, s2 = 1 + 3 * core, 4 - 3 * core
    p1, p2 = z + core * (y - z), y + core * (z - y)
    mate = {"wide": chip * 2 + 1 - core}

    def chip_peer(a1, a2):
        return {"wide": (a1 * s1 + a2 * s2) * 2 + core}

    def y_peer(step):
        return {"wide": (mod4(y + step) * RING + z) * 2 + core}

    def z_peer(step):
        return {"wide": (y * RING + mod4(z + step)) * 2 + core}

    def x_peer(step):
        return {"narrow": mod4(x + step)}

    load_sk = pltpu.make_async_copy(sk_hbm, sk_ref, local_sem.at[1])
    load_sk.start()
    load_w = pltpu.make_async_copy(w_hbm, w_ref.at[pl.ds(0, ROWS)], local_sem.at[0])
    load_w.start()

    barrier = pltpu.get_barrier_semaphore()
    peers = [mate] + [f(s) for f in (x_peer, y_peer, z_peer) for s in (1, 2, 3)]
    for peer in peers:
        pl.semaphore_signal(barrier, inc=1, device_id=peer, device_id_type=MESH)
    load_sk.wait()
    own_sk[...] = sk_ref[...].astype(F32)
    w_ref[pl.ds(ROWS, PAD - ROWS), :] = jnp.zeros((PAD - ROWS, COLS), BF16)
    pl.semaphore_wait(barrier, len(peers))

    count = [0]
    pending = []

    def send(src, dst, peer):
        at = count[0]
        count[0] += 1
        copy = pltpu.make_async_remote_copy(
            src_ref=src,
            dst_ref=dst,
            send_sem=send_sem.at[at],
            recv_sem=recv_sem.at[at],
            device_id=peer,
            device_id_type=MESH,
        )
        copy.start()
        pending.append(copy)
        return copy

    def drain():
        for copy in pending:
            copy.wait_send()
        pending.clear()

    def gather16(blk, u, v, share, meanwhile):
        (pu, su), (pv, sv) = u, v

        def at_u(step):
            return {"wide": (mod4(pu + step) * su + pv * sv) * 2 + core}

        def at_v(step):
            return {"wide": (pu * su + mod4(pv + step) * sv) * 2 + core}

        own = blk(pu, pv)
        along_u = {s: send(own, own, at_u(s)) for s in (2, 1, 3)}
        along_v = [(pu, {s: send(own, own, at_v(s)) for s in (2, 1, 3)})]
        shared = [share(pu, pv)]
        for s in (1, 3, 2):
            along_u[s].wait_recv()
            a = mod4(pu + 4 - s)
            block = blk(a, pv)
            along_v.append((a, {t: send(block, block, at_v(t)) for t in (2, 1, 3)}))
            shared.append(share(a, pv))
        for a, copies in along_v:
            for t in (1, 3, 2):
                copies[t].wait_recv()
                shared.append(share(a, mod4(pv + 4 - t)))
        meanwhile()
        for copy in shared:
            copy.wait_recv()
        drain()

    axis1, axis2 = (p1, s1), (p2, s2)
    my_off = core * SKIP
    only_off = core * WIDE
    mate_off = (1 - core) * SKIP
    my_off2, mate_off2 = core * SKIP2, (1 - core) * SKIP2

    my_cols = pl.ds(pl.multiple_of(my_off, 128), WIDE)
    first = send(own_sk.at[:, pl.ds(pl.multiple_of(mate_off, 128), WIDE)], mate_sk, mate)
    first.wait_recv()
    mine, other = own_sk[:, my_cols], mate_sk[...]
    even = core == 0
    pair = jnp.concatenate([jnp.where(even, mine, other), jnp.where(even, other, mine)], axis=0)
    s_ref[pl.ds(pl.multiple_of(chip * BLK, BLK), BLK), my_cols] = pair.astype(BF16)

    def sketch_block(a1, a2):
        return s_ref.at[pl.ds(pl.multiple_of((a1 * s1 + a2 * s2) * BLK, BLK), BLK), my_cols]

    def share_sketch(a1, a2):
        rows = pl.ds(pl.multiple_of((a1 * s1 + a2 * s2) * BLK, BLK), BLK)
        block = s_ref.at[rows, pl.ds(pl.multiple_of(only_off, 128), SKIP)]
        return send(block, block, mate)

    def rows_dot(rows, off, start, width):
        return lax.dot_general(
            w_ref[rows, pl.ds(pl.multiple_of(off + start, 128), width)],
            s_ref[:, pl.ds(pl.multiple_of(off + start, 128), width)],
            (((1,), (1,)), ((), ())),
            preferred_element_type=F32,
        )

    def own_columns():
        load_w.wait()
        part_f[...] = rows_dot(pl.ds(0, PAD), my_off, 0, WIDE)

    gather16(sketch_block, axis1, axis2, share_sketch, own_columns)
    mate_only = (1 - core) * WIDE

    def piece(step, start, size):
        return pl.ds(pl.multiple_of(mod4(x + step) * CHUNK + start, 16), size)

    def add_columns(step, start, size):
        rows = piece(step, start, size)
        value = part_f[rows, :] + rows_dot(rows, mate_only, 0, SKIP)
        part_f[rows, :] = value
        part_b[rows, :] = value.astype(BF16)

    phase = []
    for n, (start, size) in enumerate(STREAMS):
        half = size // 2
        one = {"start": start, "half": half}
        one["in"] = [img_in.at[n, k, pl.ds(0, half)] for k in range(6)]
        phase.append(one)
        add_columns(2, start, size)
        one[0] = send(part_b.at[piece(2, start, half)], one["in"][0], x_peer(1))
        one[1] = send(part_b.at[piece(2, start + half, half)], one["in"][1], x_peer(3))
    for one, (start, size) in zip(phase, STREAMS):
        half = size // 2
        add_columns(1, start, size)
        one[2] = send(part_b.at[piece(1, start + half, half)], one["in"][2], x_peer(1))
        add_columns(3, start, size)
        one[3] = send(part_b.at[piece(3, start, half)], one["in"][3], x_peer(3))
    for start, size in STREAMS:
        add_columns(0, start, size)

    def inbox(one, n, k):
        return img_in[n, k, pl.ds(0, one["half"]), :].astype(F32)

    for n, one in enumerate(phase):
        start, half = one["start"], one["half"]
        middle = pl.ds(0, half)
        one[0].wait_recv()
        img_mid[n, 0, middle, :] = (part_f[piece(1, start, half), :] + inbox(one, n, 0)).astype(BF16)
        one[4] = send(img_mid.at[n, 0, middle], one["in"][4], x_peer(1))
        one[1].wait_recv()
        img_mid[n, 1, middle, :] = (part_f[piece(3, start + half, half), :] + inbox(one, n, 1)).astype(BF16)
        one[5] = send(img_mid.at[n, 1, middle], one["in"][5], x_peer(3))

    for n, one in enumerate(phase):
        start, half = one["start"], one["half"]
        own_a, own_b = piece(0, start, half), piece(0, start + half, half)
        one[3].wait_recv()
        one[4].wait_recv()
        img[own_a, :] = (part_f[own_a, :] + inbox(one, n, 3) + inbox(one, n, 4)).astype(BF16)
        one["a_right"] = send(img.at[own_a], img.at[own_a], x_peer(1))
        one[2].wait_recv()
        one[5].wait_recv()
        img[own_b, :] = (part_f[own_b, :] + inbox(one, n, 2) + inbox(one, n, 5)).astype(BF16)
        one["b_left"] = send(img.at[own_b], img.at[own_b], x_peer(3))
        one["b_right"] = send(img.at[own_b], img.at[own_b], x_peer(1))
        one["a_left"] = send(img.at[own_a], img.at[own_a], x_peer(3))

    def pass_on(one):
        start, half = one["start"], one["half"]
        one["a_right"].wait_recv()
        rows = piece(3, start, half)
        one["opp_a"] = send(img.at[rows], img.at[rows], x_peer(1))
        one["b_left"].wait_recv()
        rows = piece(1, start + half, half)
        one["opp_b"] = send(img.at[rows], img.at[rows], x_peer(3))

    own = img[piece(0, 0, CHUNK), :]
    full = lax.dot_general(own, own, (((0,), (0,)), ((), ())), preferred_element_type=F32)
    for c in (0, 1):
        gram[c, pl.ds(0, 128), :] = full[c * 128 : c * 128 + 128, c * 128 : c * 128 + 128]
        gram[c, pl.ds(128, 64), :] = full[c * 64 : c * 64 + 64, 128:]
    copy = send(gram.at[1 - core], gram_pair, mate)
    for one in phase[:-1]:
        pass_on(one)
    copy.wait_recv()
    gram_own[...] = gram[core] + gram_pair[...]

    def gram_rows(ax):
        return pl.ds(pl.multiple_of(ax * 48, 16), 48)

    at_x = gram_rows(x)
    gram_stage = {
        s: send(gram_own.at[gram_rows(mod4(x + s))], gram_x.at[s - 1], x_peer(s)) for s in (2, 1, 3)
    }
    pass_on(phase[-1])
    for copy in gram_stage.values():
        copy.wait_recv()
    gram_z[0] = gram_own[at_x, :] + gram_x[0] + gram_x[1] + gram_x[2]
    gram_stage = [send(gram_z.at[0], gram_z.at[s], z_peer(s)) for s in (2, 1, 3)]
    for one in phase:
        for name in ("a_left", "b_right", "opp_a", "opp_b"):
            one[name].wait_recv()

    img_t[...] = img[...].T

    def group(off, a2, sa, sb):
        columns = [
            w_ref[:, pl.ds(pl.multiple_of(off + (a1 * sa + a2 * sb) * 128, 128), 128)]
            for a1 in range(RING)
        ]
        return dot(img_t[...], jnp.concatenate(columns, axis=1))

    turns = (2, 1, 3, 0)
    copies = []
    for j, s in enumerate(turns):
        mate_send[j] = group(mate_off2, mod4(p1 + s), s2, s1).astype(BF16)
        copies.append(send(mate_send.at[j], mate_recv.at[j], mate))

    scatter = []
    for j, s in enumerate(turns):
        value = group(my_off2, mod4(p2 + s), s1, s2)
        copies[j].wait_recv()
        value = value + mate_recv[j].astype(F32)
        for a1 in range(RING):
            block = value[:, a1 * 128 : a1 * 128 + 128]
            z_f[j, a1] = block
            z_b[j, a1] = block.astype(BF16)
        if j == 0:
            for copy in gram_stage:
                copy.wait_recv()
            gram_y[0] = gram_z[0] + gram_z[1] + gram_z[2] + gram_z[3]
            gram_stage = [send(gram_y.at[0], gram_y.at[t], y_peer(t)) for t in (2, 1, 3)]
        peers_u = [(t, mod4(p1 + t)) for t in (2, 1, 3)]
        scatter.append([send(z_b.at[j, a1], z_in.at[j, t - 1], chip_peer(a1, p2)) for t, a1 in peers_u])

    def row_sum(j):
        for copy in scatter[j]:
            copy.wait_recv()
        value = z_f[j, p1]
        for t in range(3):
            value = value + z_in[j, t].astype(F32)
        return value

    def send_row(j):
        s = turns[j]
        row_b[j] = row_sum(j).astype(BF16)
        return send(row_b.at[j], col_in.at[s - 1], chip_peer(p1, mod4(p2 + s)))

    for copy in gram_stage:
        copy.wait_recv()
    total[core, at_x, :] = gram_y[0] + gram_y[1] + gram_y[2] + gram_y[3]
    mine = total.at[core, at_x]
    gram_stage = [send(mine, mine, x_peer(s)) for s in (2, 1, 3)]
    column = [send_row(0), send_row(1)]
    for copy in gram_stage:
        copy.wait_recv()
    copy = send(total.at[core], total.at[core], mate)
    column.append(send_row(2))
    row_f[...] = row_sum(3)
    copy.wait_recv()

    beside = jnp.concatenate([total[0, pl.ds(128, 64), :], total[1, pl.ds(128, 64), :]], axis=0)
    top = jnp.concatenate([total[0, pl.ds(0, 128), :], beside], axis=1)
    bottom = jnp.concatenate([beside.T, total[1, pl.ds(0, 128), :]], axis=1)
    whole = jnp.concatenate([top, bottom], axis=0)
    diagonal = lax.broadcasted_iota(jnp.int32, (RANK, RANK), 0) == lax.broadcasted_iota(
        jnp.int32, (RANK, RANK), 1
    )
    trace = jnp.sum(jnp.where(diagonal, whole, 0.0), keepdims=True)
    poly[pl.ds(0, RANK), :] = whole / trace
    poly[pl.ds(RANK, RANK), :] = jnp.where(diagonal, 1.0 / jnp.sqrt(trace), 0.0)

    def factor(g):
        return jnp.where(diagonal, 1.5, 0.0) - 0.5 * g

    def step(both):
        p_high, p_low = split(factor(both[:RANK]))

        def times_p(a):
            a_high, a_low = split(a)
            return dot(a_high, p_high) + (dot(a_high, p_low) + dot(a_low, p_high))

        both = times_p(both)
        return times_p(both[:RANK]), both[RANK:]

    def iteration(_, carry):
        g, q = step(poly[...])
        poly[pl.ds(0, RANK), :] = g
        poly[pl.ds(RANK, RANK), :] = q
        return carry

    lax.fori_loop(0, ITERS - 2, iteration, 0)
    for copy in column:
        copy.wait_recv()
    mine = row_f[...]
    for s in range(3):
        mine = mine + col_in[s].astype(F32)
    g, q = step(poly[...])
    last = factor(g)
    coef_out[core, chip] = dot_split(last, dot_split(q, mine)).astype(BF16)
    poly[pl.ds(0, RANK), :] = last
    poly[pl.ds(RANK, RANK), :] = q

    def coef_block(a2, a1):
        return coef_out.at[core, a1 * s1 + a2 * s2]

    def share_coef(a2, a1):
        return send(coef_block(a2, a1), coef_block(a2, a1), mate)

    def basis_rows():
        own = img[pl.ds(0, ROWS), :]
        q_high, q_low = split(dot_split(poly[pl.ds(RANK, RANK), :], poly[pl.ds(0, RANK), :]))
        basis_out[...] = (dot(own, q_high) + dot(own, q_low)).astype(BF16)

    gather16(coef_block, axis2, axis1, share_coef, basis_rows)
    assert count[0] <= COPIES, count[0]


COPIES = 160
STEPS = (48, 96, 192, 240, 288, 288, 240)


def residual_kernel(w_ref, basis_ref, coef_ref, residual_out, own_ref, result, sem):
    def tile(at):
        return coef_ref.at[(0, at) if at < TILES else (1, at - SKIP2 // 128)]

    copies = []
    start = 0
    for n, size in enumerate(STEPS):
        rows = pl.ds(start, size)
        left = basis_ref[rows, :]
        for at in range(0, COLS // 128, 2):
            width = min(2, COLS // 128 - at)
            cols = pl.ds(at * 128, width * 128)
            right = jnp.concatenate([tile(at + k)[...] for k in range(width)], axis=1)
            result[rows, cols] = (w_ref[rows, cols].astype(F32) - dot(left, right)).astype(BF16)
        copy = pltpu.make_async_copy(result.at[rows], residual_out.at[rows], sem.at[n])
        copy.start()
        copies.append(copy)
        start += size
    wide = lax.axis_index("wide")
    rows = pl.ds(pl.multiple_of((wide // 2) * BLK, BLK), BLK)
    first = lax.rem(wide, 2) == 0
    for at in range(COLS // 128):
        block = tile(at)[rows, :].astype(F32)
        own_ref[:, at * 128 : at * 128 + 128] = jnp.where(first, block[:8], block[8:]).astype(BF16)
    for copy in copies:
        copy.wait()


def shards(weight, sketch):
    basis, coef = pl.pallas_call(
        main_kernel,
        out_shape=(
            jax.ShapeDtypeStruct((ROWS, RANK), BF16),
            jax.ShapeDtypeStruct((2, TILES, RANK, 128), BF16),
        ),
        in_specs=[pl.BlockSpec(memory_space=pltpu.HBM)] * 2,
        out_specs=[pl.BlockSpec(memory_space=pltpu.VMEM)] * 2,
        scratch_shapes=[
            pltpu.VMEM((PAD, COLS), BF16),
            pltpu.VMEM((8, COLS), BF16),
            pltpu.VMEM((8, COLS), F32),
            pltpu.VMEM((8, WIDE), F32),
            pltpu.VMEM((RANK, COLS), BF16),
            pltpu.VMEM((PAD, RANK), F32),
            pltpu.VMEM((PAD, RANK), BF16),
            pltpu.VMEM((len(STREAMS), 6, 96, RANK), BF16),
            pltpu.VMEM((len(STREAMS), 2, 96, RANK), BF16),
            pltpu.VMEM((2, 192, 128), F32),
            pltpu.VMEM((192, 128), F32),
            pltpu.VMEM((2, 192, 128), F32),
            pltpu.VMEM((192, 128), F32),
            pltpu.VMEM((3, 48, 128), F32),
            pltpu.VMEM((4, 48, 128), F32),
            pltpu.VMEM((4, 48, 128), F32),
            pltpu.VMEM((2 * RANK, RANK), F32),
            pltpu.VMEM((PAD, RANK), BF16),
            pltpu.VMEM((RANK, PAD), BF16),
            pltpu.VMEM((RING, RANK, 512), BF16),
            pltpu.VMEM((RING, RANK, 512), BF16),
            pltpu.VMEM((RING, RING, RANK, 128), F32),
            pltpu.VMEM((RING, RING, RANK, 128), BF16),
            pltpu.VMEM((RING, 3, RANK, 128), BF16),
            pltpu.VMEM((RANK, 128), F32),
            pltpu.VMEM((3, RANK, 128), BF16),
            pltpu.VMEM((3, RANK, 128), BF16),
            pltpu.SemaphoreType.DMA((2,)),
            pltpu.SemaphoreType.DMA((COPIES,)),
            pltpu.SemaphoreType.DMA((COPIES,)),
        ],
        compiler_params=pltpu.CompilerParams(
            collective_id=0, has_side_effects=True, vmem_limit_bytes=44 * 1024 * 1024
        ),
        cost_estimate=pl.CostEstimate(
            flops=2 * 2 * ROWS * COLS * RANK, bytes_accessed=2 * ROWS * COLS, transcendentals=0
        ),
        name="polar_basis",
    )(weight, pltpu.with_memory_space_constraint(sketch.T, pltpu.HBM))

    residual, own = pl.pallas_call(
        residual_kernel,
        out_shape=(
            jax.ShapeDtypeStruct((ROWS, COLS), BF16),
            jax.ShapeDtypeStruct((8, COLS), BF16),
        ),
        in_specs=[pl.BlockSpec(memory_space=pltpu.VMEM)] * 3,
        out_specs=[
            pl.BlockSpec(memory_space=pl.ANY),
            pl.BlockSpec(memory_space=pltpu.VMEM),
        ],
        scratch_shapes=[
            pltpu.VMEM((ROWS, COLS), BF16),
            pltpu.SemaphoreType.DMA((len(STEPS),)),
        ],
        compiler_params=pltpu.CompilerParams(vmem_limit_bytes=24 * 1024 * 1024),
        cost_estimate=pl.CostEstimate(
            flops=2 * ROWS * COLS * RANK, bytes_accessed=4 * ROWS * COLS, transcendentals=0
        ),
        name="residual",
    )(weight, basis, coef)
    return own, residual


def solution(mesh):
    placed = (P("wide", "narrow"), P("narrow", "wide"))
    return jax.shard_map(
        shards,
        mesh=mesh,
        in_specs=placed,
        out_specs=(P("wide", "narrow"), P("wide", "narrow")),
        check_vma=False,
    )
```

```python
import jax
import jax.numpy as jnp
from jax import lax
from jax.experimental import pallas as pl
from jax.experimental.pallas import tpu as pltpu
from jax.sharding import PartitionSpec as P

ITERS = 6
RING = 4
RANK = 256
ROWS = 1392
COLS = 3712
PAD = 1408
CHUNK = PAD // RING
STREAMS = ((0, 192), (192, 160))
BLK = 16
WIDE = 1920
SKIP = COLS - WIDE
TILES = 16
SKIP2 = COLS - TILES * 128
MESH = pl.DeviceIdType.MESH
F32 = jnp.float32
BF16 = jnp.bfloat16


def mod4(value):
    return lax.rem(value, RING)


def split(value):
    high = value.astype(BF16)
    return high, (value - high.astype(F32)).astype(BF16)


def dot(a, b):
    return jnp.dot(a, b, preferred_element_type=F32)


def dot_split(a, b):
    a_high, a_low = split(a)
    b_high, b_low = split(b)
    return dot(a_high, b_high) + (dot(a_high, b_low) + dot(a_low, b_high))


def main_kernel(
    w_hbm,
    sk_hbm,
    basis_out,
    coef_out,
    w_ref,
    sk_ref,
    own_sk,
    mate_sk,
    s_ref,
    part_f,
    part_b,
    img_in,
    img_mid,
    gram,
    gram_own,
    total,
    gram_pair,
    gram_x,
    gram_y,
    gram_z,
    poly,
    img,
    img_t,
    mate_send,
    mate_recv,
    z_f,
    z_b,
    z_in,
    row_f,
    row_b,
    col_in,
    local_sem,
    send_sem,
    recv_sem,
):
    wide = lax.axis_index("wide")
    x = lax.axis_index("narrow")
    core = lax.rem(wide, 2)
    chip = wide // 2
    y, z = chip // RING, lax.rem(chip, RING)
    s1, s2 = 1 + 3 * core, 4 - 3 * core
    p1, p2 = z + core * (y - z), y + core * (z - y)
    mate = {"wide": chip * 2 + 1 - core}

    def chip_peer(a1, a2):
        return {"wide": (a1 * s1 + a2 * s2) * 2 + core}

    def y_peer(step):
        return {"wide": (mod4(y + step) * RING + z) * 2 + core}

    def z_peer(step):
        return {"wide": (y * RING + mod4(z + step)) * 2 + core}

    def x_peer(step):
        return {"narrow": mod4(x + step)}

    load_sk = pltpu.make_async_copy(sk_hbm, sk_ref, local_sem.at[1])
    load_sk.start()
    load_w = pltpu.make_async_copy(w_hbm, w_ref.at[pl.ds(0, ROWS)], local_sem.at[0])
    load_w.start()

    barrier = pltpu.get_barrier_semaphore()
    peers = [mate] + [f(s) for f in (x_peer, y_peer, z_peer) for s in (1, 2, 3)]
    for peer in peers:
        pl.semaphore_signal(barrier, inc=1, device_id=peer, device_id_type=MESH)
    load_sk.wait()
    own_sk[...] = sk_ref[...].astype(F32)
    w_ref[pl.ds(ROWS, PAD - ROWS), :] = jnp.zeros((PAD - ROWS, COLS), BF16)
    pl.semaphore_wait(barrier, len(peers))

    count = [0]
    pending = []

    def send(src, dst, peer):
        at = count[0]
        count[0] += 1
        copy = pltpu.make_async_remote_copy(
            src_ref=src,
            dst_ref=dst,
            send_sem=send_sem.at[at],
            recv_sem=recv_sem.at[at],
            device_id=peer,
            device_id_type=MESH,
        )
        copy.start()
        pending.append(copy)
        return copy

    def drain():
        for copy in pending:
            copy.wait_send()
        pending.clear()

    def gather16(blk, u, v, share, meanwhile, early):
        (pu, su), (pv, sv) = u, v

        def at_u(step):
            return {"wide": (mod4(pu + step) * su + pv * sv) * 2 + core}

        def at_v(step):
            return {"wide": (pu * su + mod4(pv + step) * sv) * 2 + core}

        own = blk(pu, pv)
        along_u = {s: send(own, own, at_u(s)) for s in (2, 1, 3)}
        along_v = [(pu, {s: send(own, own, at_v(s)) for s in (2, 1, 3)})]
        shared = [share(pu, pv)]
        for s in (1, 3, 2):
            along_u[s].wait_recv()
            a = mod4(pu + 4 - s)
            block = blk(a, pv)
            along_v.append((a, {t: send(block, block, at_v(t)) for t in (2, 1, 3)}))
            shared.append(share(a, pv))
        early()
        for a, copies in along_v:
            for t in (1, 3, 2):
                copies[t].wait_recv()
                shared.append(share(a, mod4(pv + 4 - t)))
        meanwhile()
        for copy in shared:
            copy.wait_recv()
        drain()

    axis1, axis2 = (p1, s1), (p2, s2)
    my_off = core * SKIP
    only_off = core * WIDE
    mate_off = (1 - core) * SKIP
    my_off2, mate_off2 = core * SKIP2, (1 - core) * SKIP2

    my_cols = pl.ds(pl.multiple_of(my_off, 128), WIDE)
    first = send(own_sk.at[:, pl.ds(pl.multiple_of(mate_off, 128), WIDE)], mate_sk, mate)
    first.wait_recv()
    mine, other = own_sk[:, my_cols], mate_sk[...]
    even = core == 0
    pair = jnp.concatenate([jnp.where(even, mine, other), jnp.where(even, other, mine)], axis=0)
    s_ref[pl.ds(pl.multiple_of(chip * BLK, BLK), BLK), my_cols] = pair.astype(BF16)

    def sketch_block(a1, a2):
        return s_ref.at[pl.ds(pl.multiple_of((a1 * s1 + a2 * s2) * BLK, BLK), BLK), my_cols]

    def share_sketch(a1, a2):
        rows = pl.ds(pl.multiple_of((a1 * s1 + a2 * s2) * BLK, BLK), BLK)
        block = s_ref.at[rows, pl.ds(pl.multiple_of(only_off, 128), SKIP)]
        return send(block, block, mate)

    def rows_dot(rows, off, start, width):
        return lax.dot_general(
            w_ref[rows, pl.ds(pl.multiple_of(off + start, 128), width)],
            s_ref[:, pl.ds(pl.multiple_of(off + start, 128), width)],
            (((1,), (1,)), ((), ())),
            preferred_element_type=F32,
        )

    def own_columns():
        load_w.wait()
        part_f[...] = rows_dot(pl.ds(0, PAD), my_off, 0, WIDE)

    gather16(sketch_block, axis1, axis2, share_sketch, own_columns, lambda: None)
    mate_only = (1 - core) * WIDE

    def piece(step, start, size):
        return pl.ds(pl.multiple_of(mod4(x + step) * CHUNK + start, 16), size)

    def add_columns(step, start, size):
        rows = piece(step, start, size)
        value = part_f[rows, :] + rows_dot(rows, mate_only, 0, SKIP)
        part_f[rows, :] = value
        part_b[rows, :] = value.astype(BF16)

    phase = []
    for n, (start, size) in enumerate(STREAMS):
        half = size // 2
        one = {"start": start, "half": half}
        one["in"] = [img_in.at[n, k, pl.ds(0, half)] for k in range(6)]
        phase.append(one)
        add_columns(2, start, size)
        one[0] = send(part_b.at[piece(2, start, half)], one["in"][0], x_peer(1))
        one[1] = send(part_b.at[piece(2, start + half, half)], one["in"][1], x_peer(3))
    for one, (start, size) in zip(phase, STREAMS):
        half = size // 2
        add_columns(1, start, size)
        one[2] = send(part_b.at[piece(1, start + half, half)], one["in"][2], x_peer(1))
        add_columns(3, start, size)
        one[3] = send(part_b.at[piece(3, start, half)], one["in"][3], x_peer(3))
    for start, size in STREAMS:
        add_columns(0, start, size)

    def inbox(one, n, k):
        return img_in[n, k, pl.ds(0, one["half"]), :].astype(F32)

    for n, one in enumerate(phase):
        start, half = one["start"], one["half"]
        middle = pl.ds(0, half)
        one[0].wait_recv()
        img_mid[n, 0, middle, :] = (part_f[piece(1, start, half), :] + inbox(one, n, 0)).astype(BF16)
        one[4] = send(img_mid.at[n, 0, middle], one["in"][4], x_peer(1))
        one[1].wait_recv()
        img_mid[n, 1, middle, :] = (part_f[piece(3, start + half, half), :] + inbox(one, n, 1)).astype(BF16)
        one[5] = send(img_mid.at[n, 1, middle], one["in"][5], x_peer(3))

    for n, one in enumerate(phase):
        start, half = one["start"], one["half"]
        own_a, own_b = piece(0, start, half), piece(0, start + half, half)
        one[3].wait_recv()
        one[4].wait_recv()
        img[own_a, :] = (part_f[own_a, :] + inbox(one, n, 3) + inbox(one, n, 4)).astype(BF16)
        one["a_right"] = send(img.at[own_a], img.at[own_a], x_peer(1))
        one[2].wait_recv()
        one[5].wait_recv()
        img[own_b, :] = (part_f[own_b, :] + inbox(one, n, 2) + inbox(one, n, 5)).astype(BF16)
        one["b_left"] = send(img.at[own_b], img.at[own_b], x_peer(3))
        one["b_right"] = send(img.at[own_b], img.at[own_b], x_peer(1))
        one["a_left"] = send(img.at[own_a], img.at[own_a], x_peer(3))

    def pass_on(one):
        start, half = one["start"], one["half"]
        one["a_right"].wait_recv()
        rows = piece(3, start, half)
        one["opp_a"] = send(img.at[rows], img.at[rows], x_peer(1))
        one["b_left"].wait_recv()
        rows = piece(1, start + half, half)
        one["opp_b"] = send(img.at[rows], img.at[rows], x_peer(3))

    own = img[piece(0, 0, CHUNK), :]
    full = lax.dot_general(own, own, (((0,), (0,)), ((), ())), preferred_element_type=F32)
    for c in (0, 1):
        gram[c, pl.ds(0, 128), :] = full[c * 128 : c * 128 + 128, c * 128 : c * 128 + 128]
        gram[c, pl.ds(128, 64), :] = full[c * 64 : c * 64 + 64, 128:]
    copy = send(gram.at[1 - core], gram_pair, mate)
    for one in phase[:-1]:
        pass_on(one)
    copy.wait_recv()
    gram_own[...] = gram[core] + gram_pair[...]

    def gram_rows(ax):
        return pl.ds(pl.multiple_of(ax * 48, 16), 48)

    at_x = gram_rows(x)
    gram_stage = {
        s: send(gram_own.at[gram_rows(mod4(x + s))], gram_x.at[s - 1], x_peer(s)) for s in (2, 1, 3)
    }
    pass_on(phase[-1])
    for copy in gram_stage.values():
        copy.wait_recv()
    gram_z[0] = gram_own[at_x, :] + gram_x[0] + gram_x[1] + gram_x[2]
    gram_stage = [send(gram_z.at[0], gram_z.at[s], z_peer(s)) for s in (2, 1, 3)]
    for one in phase:
        for name in ("a_left", "b_right", "opp_a", "opp_b"):
            one[name].wait_recv()

    img_t[...] = img[...].T

    def group(off, a2, sa, sb):
        columns = [
            w_ref[:, pl.ds(pl.multiple_of(off + (a1 * sa + a2 * sb) * 128, 128), 128)]
            for a1 in range(RING)
        ]
        return dot(img_t[...], jnp.concatenate(columns, axis=1))

    turns = (2, 1, 3, 0)
    copies = []
    for j, s in enumerate(turns):
        mate_send[j] = group(mate_off2, mod4(p1 + s), s2, s1).astype(BF16)
        copies.append(send(mate_send.at[j], mate_recv.at[j], mate))

    scatter = []
    for j, s in enumerate(turns):
        value = group(my_off2, mod4(p2 + s), s1, s2)
        copies[j].wait_recv()
        value = value + mate_recv[j].astype(F32)
        for a1 in range(RING):
            block = value[:, a1 * 128 : a1 * 128 + 128]
            z_f[j, a1] = block
            z_b[j, a1] = block.astype(BF16)
        if j == 0:
            for copy in gram_stage:
                copy.wait_recv()
            gram_y[0] = gram_z[0] + gram_z[1] + gram_z[2] + gram_z[3]
            gram_stage = [send(gram_y.at[0], gram_y.at[t], y_peer(t)) for t in (2, 1, 3)]
        peers_u = [(t, mod4(p1 + t)) for t in (1, 3, 2)]
        scatter.append([send(z_b.at[j, a1], z_in.at[j, t - 1], chip_peer(a1, p2)) for t, a1 in peers_u])

    def row_sum(j):
        for copy in scatter[j]:
            copy.wait_recv()
        value = z_f[j, p1]
        for t in range(3):
            value = value + z_in[j, t].astype(F32)
        return value

    def send_row(j):
        s = turns[j]
        row_b[j] = row_sum(j).astype(BF16)
        return send(row_b.at[j], col_in.at[s - 1], chip_peer(p1, mod4(p2 + s)))

    for copy in gram_stage:
        copy.wait_recv()
    total[core, at_x, :] = gram_y[0] + gram_y[1] + gram_y[2] + gram_y[3]
    mine = total.at[core, at_x]
    gram_stage = [send(mine, mine, x_peer(s)) for s in (2, 1, 3)]
    column = [send_row(0), send_row(1)]
    for copy in gram_stage:
        copy.wait_recv()
    copy = send(total.at[core], total.at[core], mate)
    column.append(send_row(2))
    row_f[...] = row_sum(3)
    copy.wait_recv()

    beside = jnp.concatenate([total[0, pl.ds(128, 64), :], total[1, pl.ds(128, 64), :]], axis=0)
    top = jnp.concatenate([total[0, pl.ds(0, 128), :], beside], axis=1)
    bottom = jnp.concatenate([beside.T, total[1, pl.ds(0, 128), :]], axis=1)
    whole = jnp.concatenate([top, bottom], axis=0)
    diagonal = lax.broadcasted_iota(jnp.int32, (RANK, RANK), 0) == lax.broadcasted_iota(
        jnp.int32, (RANK, RANK), 1
    )
    trace = jnp.sum(jnp.where(diagonal, whole, 0.0), keepdims=True)
    poly[pl.ds(0, RANK), :] = whole / trace
    poly[pl.ds(RANK, RANK), :] = jnp.where(diagonal, 1.0 / jnp.sqrt(trace), 0.0)

    def factor(g):
        return jnp.where(diagonal, 1.5, 0.0) - 0.5 * g

    def step(both):
        p_high, p_low = split(factor(both[:RANK]))

        def times_p(a):
            a_high, a_low = split(a)
            return dot(a_high, p_high) + (dot(a_high, p_low) + dot(a_low, p_high))

        both = times_p(both)
        return times_p(both[:RANK]), both[RANK:]

    def iteration(_, carry):
        g, q = step(poly[...])
        poly[pl.ds(0, RANK), :] = g
        poly[pl.ds(RANK, RANK), :] = q
        return carry

    lax.fori_loop(0, ITERS - 2, iteration, 0)
    for copy in column:
        copy.wait_recv()
    mine = row_f[...]
    for s in range(3):
        mine = mine + col_in[s].astype(F32)
    g, q = step(poly[...])
    last = factor(g)
    coef_out[core, chip] = dot_split(last, dot_split(q, mine)).astype(BF16)
    poly[pl.ds(0, RANK), :] = last
    poly[pl.ds(RANK, RANK), :] = q

    def coef_block(a2, a1):
        return coef_out.at[core, a1 * s1 + a2 * s2]

    def share_coef(a2, a1):
        return send(coef_block(a2, a1), coef_block(a2, a1), mate)

    def basis_rows():
        own = img[pl.ds(0, ROWS), :]
        q_high, q_low = split(dot_split(poly[pl.ds(RANK, RANK), :], poly[pl.ds(0, RANK), :]))
        basis_out[...] = (dot(own, q_high) + dot(own, q_low)).astype(BF16)

    gather16(coef_block, axis2, axis1, share_coef, lambda: None, basis_rows)
    assert count[0] <= COPIES, count[0]


COPIES = 160
STEPS = (48, 96, 192, 240, 288, 288, 240)


def residual_kernel(w_ref, basis_ref, coef_ref, residual_out, own_ref, result, sem):
    def tile(at):
        return coef_ref.at[(0, at) if at < TILES else (1, at - SKIP2 // 128)]

    copies = []
    start = 0
    for n, size in enumerate(STEPS):
        rows = pl.ds(start, size)
        left = basis_ref[rows, :]
        for at in range(0, COLS // 128, 2):
            width = min(2, COLS // 128 - at)
            cols = pl.ds(at * 128, width * 128)
            right = jnp.concatenate([tile(at + k)[...] for k in range(width)], axis=1)
            result[rows, cols] = (w_ref[rows, cols].astype(F32) - dot(left, right)).astype(BF16)
        copy = pltpu.make_async_copy(result.at[rows], residual_out.at[rows], sem.at[n])
        copy.start()
        copies.append(copy)
        start += size
    wide = lax.axis_index("wide")
    rows = pl.ds(pl.multiple_of((wide // 2) * BLK, BLK), BLK)
    first = lax.rem(wide, 2) == 0
    for at in range(COLS // 128):
        block = tile(at)[rows, :].astype(F32)
        own_ref[:, at * 128 : at * 128 + 128] = jnp.where(first, block[:8], block[8:]).astype(BF16)
    for copy in copies:
        copy.wait()


def shards(weight, sketch):
    basis, coef = pl.pallas_call(
        main_kernel,
        out_shape=(
            jax.ShapeDtypeStruct((ROWS, RANK), BF16),
            jax.ShapeDtypeStruct((2, TILES, RANK, 128), BF16),
        ),
        in_specs=[pl.BlockSpec(memory_space=pltpu.HBM)] * 2,
        out_specs=[pl.BlockSpec(memory_space=pltpu.VMEM)] * 2,
        scratch_shapes=[
            pltpu.VMEM((PAD, COLS), BF16),
            pltpu.VMEM((8, COLS), BF16),
            pltpu.VMEM((8, COLS), F32),
            pltpu.VMEM((8, WIDE), F32),
            pltpu.VMEM((RANK, COLS), BF16),
            pltpu.VMEM((PAD, RANK), F32),
            pltpu.VMEM((PAD, RANK), BF16),
            pltpu.VMEM((len(STREAMS), 6, 96, RANK), BF16),
            pltpu.VMEM((len(STREAMS), 2, 96, RANK), BF16),
            pltpu.VMEM((2, 192, 128), F32),
            pltpu.VMEM((192, 128), F32),
            pltpu.VMEM((2, 192, 128), F32),
            pltpu.VMEM((192, 128), F32),
            pltpu.VMEM((3, 48, 128), F32),
            pltpu.VMEM((4, 48, 128), F32),
            pltpu.VMEM((4, 48, 128), F32),
            pltpu.VMEM((2 * RANK, RANK), F32),
            pltpu.VMEM((PAD, RANK), BF16),
            pltpu.VMEM((RANK, PAD), BF16),
            pltpu.VMEM((RING, RANK, 512), BF16),
            pltpu.VMEM((RING, RANK, 512), BF16),
            pltpu.VMEM((RING, RING, RANK, 128), F32),
            pltpu.VMEM((RING, RING, RANK, 128), BF16),
            pltpu.VMEM((RING, 3, RANK, 128), BF16),
            pltpu.VMEM((RANK, 128), F32),
            pltpu.VMEM((3, RANK, 128), BF16),
            pltpu.VMEM((3, RANK, 128), BF16),
            pltpu.SemaphoreType.DMA((2,)),
            pltpu.SemaphoreType.DMA((COPIES,)),
            pltpu.SemaphoreType.DMA((COPIES,)),
        ],
        compiler_params=pltpu.CompilerParams(
            collective_id=0, has_side_effects=True, vmem_limit_bytes=44 * 1024 * 1024
        ),
        cost_estimate=pl.CostEstimate(
            flops=2 * 2 * ROWS * COLS * RANK, bytes_accessed=2 * ROWS * COLS, transcendentals=0
        ),
        name="polar_basis",
    )(weight, pltpu.with_memory_space_constraint(sketch.T, pltpu.HBM))

    residual, own = pl.pallas_call(
        residual_kernel,
        out_shape=(
            jax.ShapeDtypeStruct((ROWS, COLS), BF16),
            jax.ShapeDtypeStruct((8, COLS), BF16),
        ),
        in_specs=[pl.BlockSpec(memory_space=pltpu.VMEM)] * 3,
        out_specs=[
            pl.BlockSpec(memory_space=pl.ANY),
            pl.BlockSpec(memory_space=pltpu.VMEM),
        ],
        scratch_shapes=[
            pltpu.VMEM((ROWS, COLS), BF16),
            pltpu.SemaphoreType.DMA((len(STEPS),)),
        ],
        compiler_params=pltpu.CompilerParams(vmem_limit_bytes=24 * 1024 * 1024),
        cost_estimate=pl.CostEstimate(
            flops=2 * ROWS * COLS * RANK, bytes_accessed=4 * ROWS * COLS, transcendentals=0
        ),
        name="residual",
    )(weight, basis, coef)
    return own, residual


def solution(mesh):
    placed = (P("wide", "narrow"), P("narrow", "wide"))
    return jax.shard_map(
        shards,
        mesh=mesh,
        in_specs=placed,
        out_specs=(P("wide", "narrow"), P("wide", "narrow")),
        check_vma=False,
    )
```

```python
import jax
import jax.numpy as jnp
from jax import lax
from jax.experimental import pallas as pl
from jax.experimental.pallas import tpu as pltpu
from jax.sharding import PartitionSpec as P

ITERS = 6
RING = 4
RANK = 256
ROWS = 1392
COLS = 3712
PAD = 1408
CHUNK = PAD // RING
STREAMS = ((0, 192), (192, 160))
BLK = 16
WIDE = 1920
SKIP = COLS - WIDE
TILES = 16
SKIP2 = COLS - TILES * 128
MESH = pl.DeviceIdType.MESH
F32 = jnp.float32
BF16 = jnp.bfloat16


def mod4(value):
    return lax.rem(value, RING)


def split(value):
    high = value.astype(BF16)
    return high, (value - high.astype(F32)).astype(BF16)


def dot(a, b):
    return jnp.dot(a, b, preferred_element_type=F32)


def dot_split(a, b):
    a_high, a_low = split(a)
    b_high, b_low = split(b)
    return dot(a_high, b_high) + (dot(a_high, b_low) + dot(a_low, b_high))


def main_kernel(
    w_hbm,
    sk_hbm,
    basis_out,
    coef_out,
    w_ref,
    sk_ref,
    own_sk,
    mate_sk,
    s_ref,
    part_f,
    part_b,
    img_in,
    img_mid,
    gram,
    gram_own,
    total,
    gram_pair,
    gram_x,
    gram_y,
    gram_z,
    poly,
    img,
    img_t,
    mate_send,
    mate_recv,
    z_f,
    z_b,
    z_in,
    row_f,
    row_b,
    col_in,
    local_sem,
    send_sem,
    recv_sem,
):
    wide = lax.axis_index("wide")
    x = lax.axis_index("narrow")
    core = lax.rem(wide, 2)
    chip = wide // 2
    y, z = chip // RING, lax.rem(chip, RING)
    s1, s2 = 1 + 3 * core, 4 - 3 * core
    p1, p2 = z + core * (y - z), y + core * (z - y)
    mate = {"wide": chip * 2 + 1 - core}

    def chip_peer(a1, a2):
        return {"wide": (a1 * s1 + a2 * s2) * 2 + core}

    def y_peer(step):
        return {"wide": (mod4(y + step) * RING + z) * 2 + core}

    def z_peer(step):
        return {"wide": (y * RING + mod4(z + step)) * 2 + core}

    def x_peer(step):
        return {"narrow": mod4(x + step)}

    load_sk = pltpu.make_async_copy(sk_hbm, sk_ref, local_sem.at[1])
    load_sk.start()
    load_w = pltpu.make_async_copy(w_hbm, w_ref.at[pl.ds(0, ROWS)], local_sem.at[0])
    load_w.start()

    barrier = pltpu.get_barrier_semaphore()
    peers = [mate] + [f(s) for f in (x_peer, y_peer, z_peer) for s in (1, 2, 3)]
    for peer in peers:
        pl.semaphore_signal(barrier, inc=1, device_id=peer, device_id_type=MESH)
    load_sk.wait()
    own_sk[...] = sk_ref[...].astype(F32)
    w_ref[pl.ds(ROWS, PAD - ROWS), :] = jnp.zeros((PAD - ROWS, COLS), BF16)
    pl.semaphore_wait(barrier, len(peers))

    count = [0]
    pending = []

    def send(src, dst, peer):
        at = count[0]
        count[0] += 1
        copy = pltpu.make_async_remote_copy(
            src_ref=src,
            dst_ref=dst,
            send_sem=send_sem.at[at],
            recv_sem=recv_sem.at[at],
            device_id=peer,
            device_id_type=MESH,
        )
        copy.start()
        pending.append(copy)
        return copy

    def drain(first=None):
        for copy in pending[:first]:
            copy.wait_send()
        del pending[:first]

    def gather16(blk, u, v, share, meanwhile, early):
        (pu, su), (pv, sv) = u, v

        def at_u(step):
            return {"wide": (mod4(pu + step) * su + pv * sv) * 2 + core}

        def at_v(step):
            return {"wide": (pu * su + mod4(pv + step) * sv) * 2 + core}

        before = len(pending)
        own = blk(pu, pv)
        along_u = {s: send(own, own, at_u(s)) for s in (2, 1, 3)}
        along_v = [(pu, {s: send(own, own, at_v(s)) for s in (2, 1, 3)})]
        shared = [share(pu, pv)]
        drain(before)
        for s in (1, 3, 2):
            along_u[s].wait_recv()
            a = mod4(pu + 4 - s)
            block = blk(a, pv)
            along_v.append((a, {t: send(block, block, at_v(t)) for t in (2, 1, 3)}))
            shared.append(share(a, pv))
        early()
        for a, copies in along_v:
            for t in (1, 3, 2):
                copies[t].wait_recv()
                shared.append(share(a, mod4(pv + 4 - t)))
        meanwhile()
        for copy in shared:
            copy.wait_recv()

    axis1, axis2 = (p1, s1), (p2, s2)
    my_off = core * SKIP
    only_off = core * WIDE
    mate_off = (1 - core) * SKIP
    my_off2, mate_off2 = core * SKIP2, (1 - core) * SKIP2

    my_cols = pl.ds(pl.multiple_of(my_off, 128), WIDE)
    first = send(own_sk.at[:, pl.ds(pl.multiple_of(mate_off, 128), WIDE)], mate_sk, mate)
    first.wait_recv()
    mine, other = own_sk[:, my_cols], mate_sk[...]
    even = core == 0
    pair = jnp.concatenate([jnp.where(even, mine, other), jnp.where(even, other, mine)], axis=0)
    s_ref[pl.ds(pl.multiple_of(chip * BLK, BLK), BLK), my_cols] = pair.astype(BF16)

    def sketch_block(a1, a2):
        return s_ref.at[pl.ds(pl.multiple_of((a1 * s1 + a2 * s2) * BLK, BLK), BLK), my_cols]

    def share_sketch(a1, a2):
        rows = pl.ds(pl.multiple_of((a1 * s1 + a2 * s2) * BLK, BLK), BLK)
        block = s_ref.at[rows, pl.ds(pl.multiple_of(only_off, 128), SKIP)]
        return send(block, block, mate)

    def rows_dot(rows, off, start, width):
        return lax.dot_general(
            w_ref[rows, pl.ds(pl.multiple_of(off + start, 128), width)],
            s_ref[:, pl.ds(pl.multiple_of(off + start, 128), width)],
            (((1,), (1,)), ((), ())),
            preferred_element_type=F32,
        )

    def own_columns():
        load_w.wait()
        part_f[...] = rows_dot(pl.ds(0, PAD), my_off, 0, WIDE)

    gather16(sketch_block, axis1, axis2, share_sketch, own_columns, lambda: None)
    mate_only = (1 - core) * WIDE
    before = len(pending)

    def piece(step, start, size):
        return pl.ds(pl.multiple_of(mod4(x + step) * CHUNK + start, 16), size)

    def add_columns(step, start, size):
        rows = piece(step, start, size)
        value = part_f[rows, :] + rows_dot(rows, mate_only, 0, SKIP)
        part_f[rows, :] = value
        part_b[rows, :] = value.astype(BF16)

    phase = []
    for n, (start, size) in enumerate(STREAMS):
        half = size // 2
        one = {"start": start, "half": half}
        one["in"] = [img_in.at[n, k, pl.ds(0, half)] for k in range(6)]
        phase.append(one)
        add_columns(2, start, size)
        one[0] = send(part_b.at[piece(2, start, half)], one["in"][0], x_peer(1))
        one[1] = send(part_b.at[piece(2, start + half, half)], one["in"][1], x_peer(3))
    for one, (start, size) in zip(phase, STREAMS):
        half = size // 2
        add_columns(1, start, size)
        one[2] = send(part_b.at[piece(1, start + half, half)], one["in"][2], x_peer(1))
        add_columns(3, start, size)
        one[3] = send(part_b.at[piece(3, start, half)], one["in"][3], x_peer(3))
    for start, size in STREAMS:
        add_columns(0, start, size)
    drain(before)

    def inbox(one, n, k):
        return img_in[n, k, pl.ds(0, one["half"]), :].astype(F32)

    for n, one in enumerate(phase):
        start, half = one["start"], one["half"]
        middle = pl.ds(0, half)
        one[0].wait_recv()
        img_mid[n, 0, middle, :] = (part_f[piece(1, start, half), :] + inbox(one, n, 0)).astype(BF16)
        one[4] = send(img_mid.at[n, 0, middle], one["in"][4], x_peer(1))
        one[1].wait_recv()
        img_mid[n, 1, middle, :] = (part_f[piece(3, start + half, half), :] + inbox(one, n, 1)).astype(BF16)
        one[5] = send(img_mid.at[n, 1, middle], one["in"][5], x_peer(3))

    for n, one in enumerate(phase):
        start, half = one["start"], one["half"]
        own_a, own_b = piece(0, start, half), piece(0, start + half, half)
        one[3].wait_recv()
        one[4].wait_recv()
        img[own_a, :] = (part_f[own_a, :] + inbox(one, n, 3) + inbox(one, n, 4)).astype(BF16)
        one["a_right"] = send(img.at[own_a], img.at[own_a], x_peer(1))
        one[2].wait_recv()
        one[5].wait_recv()
        img[own_b, :] = (part_f[own_b, :] + inbox(one, n, 2) + inbox(one, n, 5)).astype(BF16)
        one["b_left"] = send(img.at[own_b], img.at[own_b], x_peer(3))
        one["b_right"] = send(img.at[own_b], img.at[own_b], x_peer(1))
        one["a_left"] = send(img.at[own_a], img.at[own_a], x_peer(3))

    def pass_on(one):
        start, half = one["start"], one["half"]
        one["a_right"].wait_recv()
        rows = piece(3, start, half)
        one["opp_a"] = send(img.at[rows], img.at[rows], x_peer(1))
        one["b_left"].wait_recv()
        rows = piece(1, start + half, half)
        one["opp_b"] = send(img.at[rows], img.at[rows], x_peer(3))

    own = img[piece(0, 0, CHUNK), :]
    full = lax.dot_general(own, own, (((0,), (0,)), ((), ())), preferred_element_type=F32)
    for c in (0, 1):
        gram[c, pl.ds(0, 128), :] = full[c * 128 : c * 128 + 128, c * 128 : c * 128 + 128]
        gram[c, pl.ds(128, 64), :] = full[c * 64 : c * 64 + 64, 128:]
    copy = send(gram.at[1 - core], gram_pair, mate)
    for one in phase[:-1]:
        pass_on(one)
    copy.wait_recv()
    gram_own[...] = gram[core] + gram_pair[...]

    def gram_rows(ax):
        return pl.ds(pl.multiple_of(ax * 48, 16), 48)

    at_x = gram_rows(x)
    gram_stage = {
        s: send(gram_own.at[gram_rows(mod4(x + s))], gram_x.at[s - 1], x_peer(s)) for s in (2, 1, 3)
    }
    pass_on(phase[-1])
    for copy in gram_stage.values():
        copy.wait_recv()
    gram_z[0] = gram_own[at_x, :] + gram_x[0] + gram_x[1] + gram_x[2]
    gram_stage = [send(gram_z.at[0], gram_z.at[s], z_peer(s)) for s in (2, 1, 3)]
    for one in phase:
        for name in ("a_left", "b_right", "opp_a", "opp_b"):
            one[name].wait_recv()

    img_t[...] = img[...].T

    def group(off, a2, sa, sb):
        columns = [
            w_ref[:, pl.ds(pl.multiple_of(off + (a1 * sa + a2 * sb) * 128, 128), 128)]
            for a1 in range(RING)
        ]
        return dot(img_t[...], jnp.concatenate(columns, axis=1))

    turns = (2, 1, 3, 0)
    copies = []
    for j, s in enumerate(turns):
        mate_send[j] = group(mate_off2, mod4(p1 + s), s2, s1).astype(BF16)
        copies.append(send(mate_send.at[j], mate_recv.at[j], mate))

    scatter = []
    for j, s in enumerate(turns):
        value = group(my_off2, mod4(p2 + s), s1, s2)
        copies[j].wait_recv()
        value = value + mate_recv[j].astype(F32)
        for a1 in range(RING):
            block = value[:, a1 * 128 : a1 * 128 + 128]
            z_f[j, a1] = block
            z_b[j, a1] = block.astype(BF16)
        if j == 0:
            for copy in gram_stage:
                copy.wait_recv()
            gram_y[0] = gram_z[0] + gram_z[1] + gram_z[2] + gram_z[3]
            gram_stage = [send(gram_y.at[0], gram_y.at[t], y_peer(t)) for t in (2, 1, 3)]
        peers_u = [(t, mod4(p1 + t)) for t in (1, 3, 2)]
        scatter.append([send(z_b.at[j, a1], z_in.at[j, t - 1], chip_peer(a1, p2)) for t, a1 in peers_u])

    def row_sum(j):
        for copy in scatter[j]:
            copy.wait_recv()
        value = z_f[j, p1]
        for t in range(3):
            value = value + z_in[j, t].astype(F32)
        return value

    def send_row(j):
        s = turns[j]
        row_b[j] = row_sum(j).astype(BF16)
        return send(row_b.at[j], col_in.at[s - 1], chip_peer(p1, mod4(p2 + s)))

    for copy in gram_stage:
        copy.wait_recv()
    total[core, at_x, :] = gram_y[0] + gram_y[1] + gram_y[2] + gram_y[3]
    mine = total.at[core, at_x]
    gram_stage = [send(mine, mine, x_peer(s)) for s in (2, 1, 3)]
    column = [send_row(0), send_row(1)]
    for copy in gram_stage:
        copy.wait_recv()
    copy = send(total.at[core], total.at[core], mate)
    column.append(send_row(2))
    row_f[...] = row_sum(3)
    copy.wait_recv()

    beside = jnp.concatenate([total[0, pl.ds(128, 64), :], total[1, pl.ds(128, 64), :]], axis=0)
    top = jnp.concatenate([total[0, pl.ds(0, 128), :], beside], axis=1)
    bottom = jnp.concatenate([beside.T, total[1, pl.ds(0, 128), :]], axis=1)
    whole = jnp.concatenate([top, bottom], axis=0)
    diagonal = lax.broadcasted_iota(jnp.int32, (RANK, RANK), 0) == lax.broadcasted_iota(
        jnp.int32, (RANK, RANK), 1
    )
    trace = jnp.sum(jnp.where(diagonal, whole, 0.0), keepdims=True)
    poly[pl.ds(0, RANK), :] = whole / trace
    poly[pl.ds(RANK, RANK), :] = jnp.where(diagonal, 1.0 / jnp.sqrt(trace), 0.0)

    def factor(g):
        return jnp.where(diagonal, 1.5, 0.0) - 0.5 * g

    def step(both):
        p_high, p_low = split(factor(both[:RANK]))

        def times_p(a):
            a_high, a_low = split(a)
            return dot(a_high, p_high) + (dot(a_high, p_low) + dot(a_low, p_high))

        both = times_p(both)
        return times_p(both[:RANK]), both[RANK:]

    def iteration(_, carry):
        g, q = step(poly[...])
        poly[pl.ds(0, RANK), :] = g
        poly[pl.ds(RANK, RANK), :] = q
        return carry

    lax.fori_loop(0, ITERS - 2, iteration, 0)
    for copy in column:
        copy.wait_recv()
    mine = row_f[...]
    for s in range(3):
        mine = mine + col_in[s].astype(F32)
    g, q = step(poly[...])
    last = factor(g)
    coef_out[core, chip] = dot_split(last, dot_split(q, mine)).astype(BF16)
    poly[pl.ds(0, RANK), :] = last
    poly[pl.ds(RANK, RANK), :] = q

    def coef_block(a2, a1):
        return coef_out.at[core, a1 * s1 + a2 * s2]

    def share_coef(a2, a1):
        return send(coef_block(a2, a1), coef_block(a2, a1), mate)

    def basis_rows():
        own = img[pl.ds(0, ROWS), :]
        q_high, q_low = split(dot_split(poly[pl.ds(RANK, RANK), :], poly[pl.ds(0, RANK), :]))
        basis_out[...] = (dot(own, q_high) + dot(own, q_low)).astype(BF16)

    gather16(coef_block, axis2, axis1, share_coef, drain, basis_rows)
    assert count[0] <= COPIES, count[0]


COPIES = 160
STEPS = (48, 96, 192, 240, 288, 288, 240)


def residual_kernel(w_ref, basis_ref, coef_ref, residual_out, own_ref, result, sem):
    def tile(at):
        return coef_ref.at[(0, at) if at < TILES else (1, at - SKIP2 // 128)]

    copies = []
    start = 0
    for n, size in enumerate(STEPS):
        rows = pl.ds(start, size)
        left = basis_ref[rows, :]
        for at in range(0, COLS // 128, 2):
            width = min(2, COLS // 128 - at)
            cols = pl.ds(at * 128, width * 128)
            right = jnp.concatenate([tile(at + k)[...] for k in range(width)], axis=1)
            result[rows, cols] = (w_ref[rows, cols].astype(F32) - dot(left, right)).astype(BF16)
        copy = pltpu.make_async_copy(result.at[rows], residual_out.at[rows], sem.at[n])
        copy.start()
        copies.append(copy)
        start += size
    wide = lax.axis_index("wide")
    rows = pl.ds(pl.multiple_of((wide // 2) * BLK, BLK), BLK)
    first = lax.rem(wide, 2) == 0
    for at in range(COLS // 128):
        block = tile(at)[rows, :].astype(F32)
        own_ref[:, at * 128 : at * 128 + 128] = jnp.where(first, block[:8], block[8:]).astype(BF16)
    for copy in copies:
        copy.wait()


def shards(weight, sketch):
    basis, coef = pl.pallas_call(
        main_kernel,
        out_shape=(
            jax.ShapeDtypeStruct((ROWS, RANK), BF16),
            jax.ShapeDtypeStruct((2, TILES, RANK, 128), BF16),
        ),
        in_specs=[pl.BlockSpec(memory_space=pltpu.HBM)] * 2,
        out_specs=[pl.BlockSpec(memory_space=pltpu.VMEM)] * 2,
        scratch_shapes=[
            pltpu.VMEM((PAD, COLS), BF16),
            pltpu.VMEM((8, COLS), BF16),
            pltpu.VMEM((8, COLS), F32),
            pltpu.VMEM((8, WIDE), F32),
            pltpu.VMEM((RANK, COLS), BF16),
            pltpu.VMEM((PAD, RANK), F32),
            pltpu.VMEM((PAD, RANK), BF16),
            pltpu.VMEM((len(STREAMS), 6, 96, RANK), BF16),
            pltpu.VMEM((len(STREAMS), 2, 96, RANK), BF16),
            pltpu.VMEM((2, 192, 128), F32),
            pltpu.VMEM((192, 128), F32),
            pltpu.VMEM((2, 192, 128), F32),
            pltpu.VMEM((192, 128), F32),
            pltpu.VMEM((3, 48, 128), F32),
            pltpu.VMEM((4, 48, 128), F32),
            pltpu.VMEM((4, 48, 128), F32),
            pltpu.VMEM((2 * RANK, RANK), F32),
            pltpu.VMEM((PAD, RANK), BF16),
            pltpu.VMEM((RANK, PAD), BF16),
            pltpu.VMEM((RING, RANK, 512), BF16),
            pltpu.VMEM((RING, RANK, 512), BF16),
            pltpu.VMEM((RING, RING, RANK, 128), F32),
            pltpu.VMEM((RING, RING, RANK, 128), BF16),
            pltpu.VMEM((RING, 3, RANK, 128), BF16),
            pltpu.VMEM((RANK, 128), F32),
            pltpu.VMEM((3, RANK, 128), BF16),
            pltpu.VMEM((3, RANK, 128), BF16),
            pltpu.SemaphoreType.DMA((2,)),
            pltpu.SemaphoreType.DMA((COPIES,)),
            pltpu.SemaphoreType.DMA((COPIES,)),
        ],
        compiler_params=pltpu.CompilerParams(
            collective_id=0, has_side_effects=True, vmem_limit_bytes=44 * 1024 * 1024
        ),
        cost_estimate=pl.CostEstimate(
            flops=2 * 2 * ROWS * COLS * RANK, bytes_accessed=2 * ROWS * COLS, transcendentals=0
        ),
        name="polar_basis",
    )(weight, pltpu.with_memory_space_constraint(sketch.T, pltpu.HBM))

    residual, own = pl.pallas_call(
        residual_kernel,
        out_shape=(
            jax.ShapeDtypeStruct((ROWS, COLS), BF16),
            jax.ShapeDtypeStruct((8, COLS), BF16),
        ),
        in_specs=[pl.BlockSpec(memory_space=pltpu.VMEM)] * 3,
        out_specs=[
            pl.BlockSpec(memory_space=pl.ANY),
            pl.BlockSpec(memory_space=pltpu.VMEM),
        ],
        scratch_shapes=[
            pltpu.VMEM((ROWS, COLS), BF16),
            pltpu.SemaphoreType.DMA((len(STEPS),)),
        ],
        compiler_params=pltpu.CompilerParams(vmem_limit_bytes=24 * 1024 * 1024),
        cost_estimate=pl.CostEstimate(
            flops=2 * ROWS * COLS * RANK, bytes_accessed=4 * ROWS * COLS, transcendentals=0
        ),
        name="residual",
    )(weight, basis, coef)
    return own, residual


def solution(mesh):
    placed = (P("wide", "narrow"), P("narrow", "wide"))
    return jax.shard_map(
        shards,
        mesh=mesh,
        in_specs=placed,
        out_specs=(P("wide", "narrow"), P("wide", "narrow")),
        check_vma=False,
    )
```
